32 devices in a mesh: src: 4 (over z), vol: 8 (over y, x, core).
Axes of the slice: x: 2, y: 2, z: 4, core: 2. Of those that a mesh axis runs over, the one named last changes fastest.
Arguments:
- forward: bfloat16 [4096, 36, 512], P(('src', 'vol')), may hold values from -6 to 6
- item_tx: int32 [4096], P(('src', 'vol')), may hold values from 0 to 15, as said below
- item_brick: int32 [4096], P(('src', 'vol')), may hold values from 0 to 255
- tx_place: int32 [16], replicated, may hold values from 0 to 15, as said below
- brick_place: int32 [256], replicated, may hold values from 0 to 255, as said below
- adjoint: bfloat16 [16, 256, 36, 512], P('src', 'vol'), may hold values from -6 to 6
Outputs:
- gradient: float32 [2, 64, 16, 128], P(None, 'vol')
The draws below stay inside these ranges and needn't reach their ends.
Inputs may be any that keep to these rules, and one draw needn't show every extreme that they name: Stored brick i goes to owner (tx_place[item_tx[i]] // 4, brick_place[item_brick[i]] // 32) as (src index, vol index). Among the stored bricks of one device at most 8 share an owner; in every draw one owner receives exactly 8 from every device. `tx_place`: A permutation. `brick_place`: A permutation.
All inputs are finite; a program needn't handle non-finite values.
Results may differ from the reference program's by a relative error of at most 0.0003.
Values may be sent and summed in bfloat16 or wider, within the bound.
A program may use at most 128 MiB of HBM per device.

```python
import math
import jax
import jax.numpy as jnp
from jax import lax

E = 8
CELLS = 512
NFREQ = 6
CH = 36
NBY = 2
NBZ = 16
BR_OWN = 32
TX_DEV = 4
STORE = 128
CAP = 8
NTX = 16
NBRICKS = 256
NX = 64
NY = 16
NZ = 128
N_VOL = 8
DEVICES = 32


def layout(key):
    base_key = jax.random.fold_in(key, 11)
    key_list = jax.random.split(base_key, 4)
    brick_place = jax.random.permutation(key_list[0], NBRICKS).astype(jnp.int32)
    tx_place = jax.random.permutation(key_list[1], NTX).astype(jnp.int32)
    brick_of = jnp.zeros((NBRICKS,), jnp.int32).at[brick_place].set(jnp.arange(NBRICKS, dtype=jnp.int32))
    tx_of = jnp.zeros((NTX,), jnp.int32).at[tx_place].set(jnp.arange(NTX, dtype=jnp.int32))
    hottest = jax.random.randint(key_list[2], (), 0, DEVICES).astype(jnp.int32)

    def one_device(device_key):
        sub_keys = jax.random.split(device_key, 4)
        spare_slots = jax.random.permutation(sub_keys[0], (DEVICES - 1) * CAP)[:STORE - CAP].astype(jnp.int32)
        others = spare_slots // CAP
        others = others + (others >= hottest).astype(jnp.int32)
        destination = jnp.concatenate([jnp.zeros((CAP,), jnp.int32) + hottest, others])
        local_tx = jax.random.randint(sub_keys[1], (STORE,), 0, TX_DEV).astype(jnp.int32)
        local_brick = jax.random.randint(sub_keys[2], (STORE,), 0, BR_OWN).astype(jnp.int32)
        tx_ids = tx_of[destination // N_VOL * TX_DEV + local_tx]
        brick_ids = brick_of[destination % N_VOL * BR_OWN + local_brick]
        shuffle = jax.random.permutation(sub_keys[3], STORE)
        return (tx_ids[shuffle], brick_ids[shuffle])
    tx_ids, brick_ids = jax.vmap(one_device)(jax.random.split(key_list[3], DEVICES))
    return (tx_ids.reshape(-1), brick_ids.reshape(-1), tx_place, brick_place)


def draw_item_tx(key, part):
    return layout(key)[0]


def draw_item_brick(key, part):
    return layout(key)[1]


def draw_tx_place(key, part):
    return layout(key)[2]


def draw_brick_place(key, part):
    return layout(key)[3]


def block_scale(stream_key, shape, shards, low, largest):
    gain = 1.0
    for axis_at, parts in shards:
        steps = jax.random.uniform(jax.random.fold_in(jax.random.fold_in(stream_key, 6), axis_at), (parts,), jnp.float32, low / len(shards), largest / len(shards))
        gain = gain * jnp.repeat(jnp.exp(steps), shape[axis_at] // parts).reshape((-1,) + (1,) * (len(shape) - 1 - axis_at))
    return gain


def noise(stream_key, shape, spread, reach, cuts=(), kind=jnp.bfloat16):
    loudness = block_scale(stream_key, shape, cuts, -0.22, 0.18) if cuts else 1.0
    entries = jax.random.normal(stream_key, shape, jnp.float32) * spread * loudness
    return jnp.minimum(jnp.maximum(entries, -reach), reach).astype(kind)


def setup_inputs(seed: int = 0) -> dict:
    seeds = jax.random.split(jax.random.key(seed), 7)
    forward = noise(seeds[0], (DEVICES * STORE, CH, CELLS), 1.0, 6.0, ((0, 32),))
    item_tx = draw_item_tx(jax.random.fold_in(seeds[6], 71), 0)
    item_brick = draw_item_brick(jax.random.fold_in(seeds[6], 71), 0)
    tx_place = draw_tx_place(jax.random.fold_in(seeds[6], 71), 0)
    brick_place = draw_brick_place(jax.random.fold_in(seeds[6], 71), 0)
    adjoint = noise(seeds[5], (NTX, NBRICKS, CH, CELLS), 1.0, 6.0, ((0, 4), (1, 8)))
    return dict(forward=forward, item_tx=item_tx, item_brick=item_brick, tx_place=tx_place, brick_place=brick_place, adjoint=adjoint)


def tap_weights():
    raw_taps = [math.exp(-(offset - 4) * (offset - 4) / 4.5) for offset in range(9)]
    tap_total = sum(raw_taps)
    return [tap_value / tap_total for tap_value in raw_taps]


def correlate(fwd_field, adj_field):
    lead_shape = fwd_field.shape[:-2]
    fwd_split = fwd_field.reshape(lead_shape + (NFREQ, 3, 2, fwd_field.shape[-1]))
    adj_split = adj_field.reshape(lead_shape + (NFREQ, 3, 2, adj_field.shape[-1]))
    products = fwd_split[..., 0, :] * adj_split[..., 0, :] - fwd_split[..., 1, :] * adj_split[..., 1, :]
    horizontal = jnp.sum(products[..., 0:2, :], axis=(-3, -2))
    vertical = jnp.sum(products[..., 2, :], axis=-2)
    return jnp.stack([horizontal, vertical], axis=-2)


def smooth_axis(padded, axis):
    weights = tap_weights()
    length = padded.shape[axis] - 8
    summed = jnp.zeros(padded.shape[:axis] + (length,) + padded.shape[axis + 1:], jnp.float32)
    for offset in range(9):
        summed = summed + weights[offset] * lax.slice_in_dim(padded, offset, offset + length, axis=axis)
    return summed


def pad_axis(field, axis):
    widths = [(0, 0)] * field.ndim
    widths[axis] = (4, 4)
    return jnp.pad(field, widths)


def reference(forward, item_tx, item_brick, tx_place, brick_place, adjoint):
    tx_at = tx_place[item_tx].astype(jnp.int32)
    brick_at = brick_place[item_brick].astype(jnp.int32)
    fwd_blocks = forward.reshape(DEVICES, STORE, CH, CELLS)

    def step(gradient, block_items):
        fwd_part, tx_part, brick_part = block_items
        picked = adjoint[tx_part, brick_part]
        product = correlate(fwd_part.astype(jnp.float32), picked.astype(jnp.float32))
        return gradient.at[brick_part].add(product), None

    start = jnp.zeros((NBRICKS, 2, CELLS), jnp.float32)
    raw, _ = lax.scan(step, start, (fwd_blocks, tx_at.reshape(DEVICES, STORE), brick_at.reshape(DEVICES, STORE)))
    field = raw.reshape(N_VOL, NBY, NBZ, 2, E, E, E).transpose(3, 0, 4, 1, 5, 2, 6).reshape(2, NX, NY, NZ)
    for axis in (1, 2, 3):
        field = smooth_axis(pad_axis(field, axis), axis)
    return field
```

```python
import functools
import math

import jax
import jax.numpy as jnp
from jax import lax
from jax.experimental import pallas as pl
from jax.experimental.pallas import tpu as pltpu
from jax.sharding import PartitionSpec as P

E = 8
NBY = 2
NBZ = 16
GROUP = 4
DIRECT = 4
SPILL = 16
PARAMS = pltpu.CompilerParams(vmem_limit_bytes=48 * 1024 * 1024)


def with_halo(cells, sides, width):
    for axis, dim in sides:
        count = lax.axis_size(axis)
        ends = count - 1
        head = lax.slice_in_dim(cells, 0, width, axis=dim)
        tail = lax.slice_in_dim(cells, cells.shape[dim] - width, cells.shape[dim], axis=dim)
        cells = jnp.concatenate(
            [
                lax.ppermute(tail, axis, [(i, (i + 1) % count) for i in range(ends)]),
                cells,
                lax.ppermute(head, axis, [((i + 1) % count, i) for i in range(ends)]),
            ],
            axis=dim,
        )
    return cells


def tap_weights():
    raw_taps = [math.exp(-(offset - 4) * (offset - 4) / 4.5) for offset in range(9)]
    tap_total = sum(raw_taps)
    return [tap_value / tap_total for tap_value in raw_taps]


def smooth_axis(padded, axis):
    weights = tap_weights()
    length = padded.shape[axis] - 8
    summed = jnp.zeros(padded.shape[:axis] + (length,) + padded.shape[axis + 1 :], jnp.float32)
    for offset in range(9):
        summed = summed + weights[offset] * lax.slice_in_dim(
            padded, offset, offset + length, axis=axis
        )
    return summed


def pad_axis(field, axis):
    widths = [(0, 0)] * field.ndim
    widths[axis] = (4, 4)
    return jnp.pad(field, widths)


def lookup(indices, table):
    hits = indices[:, None] == jnp.arange(table.shape[0], dtype=jnp.int32)[None, :]
    return jnp.sum(jnp.where(hits, table[None, :], 0), axis=1)


def place(slots, values, total):
    hits = slots[None, :] == jnp.arange(total, dtype=jnp.int32)[:, None]
    return jnp.sum(jnp.where(hits, values[None, :] + 1, 0), axis=1) - 1


def same_channel(table, row_axis, column_axis):
    table = jnp.expand_dims(table, (row_axis, column_axis))
    shape = [1] * table.ndim
    shape[row_axis] = shape[column_axis] = GROUP
    return table & jnp.eye(GROUP, dtype=bool).reshape(shape)


def route_body(table_ref, cells_ref, out_ref):
    rows = cells_ref[...].reshape(-1, cells_ref.shape[-1])
    moved = jnp.dot(table_ref[...], rows, preferred_element_type=jnp.float32)
    out_ref[...] = moved.astype(out_ref.dtype).reshape(out_ref.shape)


def route(table, cells, spec, parts):
    groups = cells.shape[0] // GROUP if cells.ndim == 3 else cells.shape[1]
    rows = table.shape[0] // parts
    width = cells.shape[-1]
    return pl.pallas_call(
        route_body,
        grid=(groups,),
        in_specs=[pl.BlockSpec(table.shape, lambda g: (0, 0)), spec],
        out_specs=pl.BlockSpec((parts, 1, rows, width), lambda g: (0, g, 0, 0)),
        out_shape=jax.ShapeDtypeStruct((parts, groups, rows, width), cells.dtype),
        compiler_params=PARAMS,
    )(table, cells)


def pack(table, forward, parts):
    slots, stored = table.shape[1:]
    table = same_channel(table, 1, 3).astype(forward.dtype)
    table = table.reshape(parts * GROUP * slots, GROUP * stored)
    spec = pl.BlockSpec((GROUP,) + forward.shape[1:], lambda g: (g, 0, 0))
    return route(table, forward, spec, parts)


def reduce_body(count, *refs):
    tables, blocks, adjoint_ref, out_ref = refs[:count], refs[count : 2 * count], refs[-2], refs[-1]
    step = pl.program_id(0)
    local_tx, _, bricks, width = adjoint_ref.shape

    @pl.when(step == 0)
    def _():
        out_ref[...] = jnp.zeros_like(out_ref)

    summed = 0.0
    for table_ref, block_ref in zip(tables, blocks):
        rows = block_ref[...].reshape(-1, width)
        summed += jnp.dot(table_ref[...], rows, preferred_element_type=jnp.float32)
    summed = summed.reshape(GROUP, local_tx, bricks, width)
    for pair in range(GROUP // 2):
        total = 0.0
        for tx in range(local_tx):
            real = adjoint_ref[tx, 2 * pair].astype(jnp.float32)
            imag = adjoint_ref[tx, 2 * pair + 1].astype(jnp.float32)
            total += summed[2 * pair, tx] * real - summed[2 * pair + 1, tx] * imag
        vertical = lax.rem(step * (GROUP // 2) + pair, 3) == 2
        out_ref[0] += jnp.where(vertical, 0.0, total)
        out_ref[1] += jnp.where(vertical, total, 0.0)


def reduce(tables, blocks, adjoint):
    local_tx, channels, bricks, width = adjoint.shape
    flat = []
    for table in tables:
        last = table.ndim
        wide = same_channel(table, 0, last).astype(adjoint.dtype)
        flat.append(wide.reshape(GROUP * table.shape[0], -1))
    block_specs = [
        pl.BlockSpec((block.shape[0], 1) + block.shape[2:], lambda g: (0, g, 0, 0))
        for block in blocks
    ]
    return pl.pallas_call(
        functools.partial(reduce_body, len(flat)),
        grid=(channels // GROUP,),
        in_specs=[pl.BlockSpec(table.shape, lambda g: (0, 0)) for table in flat]
        + block_specs
        + [pl.BlockSpec((local_tx, GROUP, bricks, width), lambda g: (0, g, 0, 0))],
        out_specs=pl.BlockSpec((2, bricks, width), lambda g: (0, 0, 0)),
        out_shape=jax.ShapeDtypeStruct((2, bricks, width), jnp.float32),
        compiler_params=PARAMS,
    )(*flat, *blocks, adjoint)


def local(forward, item_tx, item_brick, tx_place, brick_place, adjoint):
    stored = forward.shape[0]
    src_count = lax.axis_size("src")
    vol_count = lax.axis_size("vol")
    devices = src_count * vol_count
    local_tx, local_bricks = adjoint.shape[:2]
    pairs = local_tx * local_bricks
    capacity = max(2, 2 * stored // devices)
    ranks = -(-max(capacity, DIRECT) // DIRECT) * DIRECT
    further = ranks - DIRECT
    both = ("src", "vol")

    tx_at = lookup(item_tx, tx_place)
    brick_at = lookup(item_brick, brick_place)
    plane = tx_at // local_tx
    column = brick_at // local_bricks
    owner = plane * vol_count + column
    pair = tx_at % local_tx * local_bricks + brick_at % local_bricks
    positions = jnp.arange(stored, dtype=jnp.int32)
    earlier = positions[:, None] > positions[None, :]
    rank = jnp.sum((owner[:, None] == owner[None, :]) & earlier, axis=1, dtype=jnp.int32)
    spilled = rank >= DIRECT
    before = earlier & spilled[None, :] & (plane[:, None] == plane[None, :])
    spill_rank = jnp.sum(before, axis=1, dtype=jnp.int32)
    late = spilled & (spill_rank >= SPILL)
    via = spilled & ~late

    channel_major = forward.transpose(1, 0, 2)
    adjoint_major = adjoint.transpose(0, 2, 1, 3)
    slot_ids = jnp.arange(DIRECT, dtype=jnp.int32)
    owner_ids = jnp.arange(devices, dtype=jnp.int32)
    pair_ids = jnp.arange(pairs, dtype=jnp.int32)

    listed = place(owner * ranks + rank, pair * 2 + late, devices * ranks)
    notes = [listed.reshape(src_count, vol_count, ranks)]
    if further:
        spill_slot = jnp.where(via, plane * SPILL + spill_rank, -1)
        codes = place(spill_slot, column * further + rank - DIRECT, src_count * SPILL)
        codes = codes.reshape(src_count, 1, SPILL)
        notes.append(jnp.broadcast_to(codes, (src_count, vol_count, SPILL)))
        any_late = jnp.max(late.astype(jnp.int32))
        notes.append(jnp.broadcast_to(any_late, (src_count, vol_count, 1)))
    notes = jnp.concatenate(notes, axis=2).reshape(devices, -1)
    notes = lax.all_to_all(notes, both, split_axis=0, concat_axis=0, tiled=True)
    notes = notes.reshape(src_count, vol_count, -1)
    listed = notes[..., :ranks]
    held = jnp.where((listed >= 0) & (listed % 2 == 0), listed // 2, -1)
    held_late = jnp.where((listed >= 0) & (listed % 2 == 1), listed // 2, -1)

    def send_direct(chosen, first):
        wanted = owner_ids[:, None] * DIRECT + slot_ids[None, :]
        slot = jnp.where(chosen, owner * DIRECT + rank - first, -1)
        packed = pack(wanted[:, :, None] == slot[None, None, :], channel_major, devices)
        return lax.all_to_all(packed, both, split_axis=0, concat_axis=0, tiled=True)

    def table_of(held_pairs):
        return held_pairs[None] == pair_ids.reshape((-1,) + (1,) * held_pairs.ndim)

    tables, blocks = [], []
    if further:
        wanted = jnp.arange(src_count * SPILL, dtype=jnp.int32).reshape(src_count, SPILL)
        packed = pack(wanted[:, :, None] == spill_slot[None, None, :], channel_major, src_count)
        spill = lax.all_to_all(packed, "src", split_axis=0, concat_axis=0, tiled=True)
    tables.append(table_of(held[..., :DIRECT].reshape(devices, DIRECT)))
    direct = send_direct(~spilled, 0)
    if further:
        codes = lax.dynamic_index_in_dim(notes, lax.axis_index("vol"), 1, keepdims=False)
        codes = codes[:, ranks : ranks + SPILL]
        wanted = jnp.arange(vol_count * further, dtype=jnp.int32).reshape(vol_count, 1, further, 1)
        table = wanted == codes[None, :, None, :]
        table = table[:, :, :, None, :] & jnp.eye(src_count, dtype=bool)[None, :, None, :, None]
        table = same_channel(table, 2, 5).astype(forward.dtype)
        table = table.reshape(vol_count * src_count * GROUP * further, -1)
        spec = pl.BlockSpec((src_count, 1) + spill.shape[2:], lambda g: (0, g, 0, 0))
        packed = route(table, spill, spec, vol_count)
        rest = lax.all_to_all(packed, "vol", split_axis=0, concat_axis=0, tiled=True)
        tables.append(table_of(held[..., DIRECT:].swapaxes(0, 1)))
        blocks.append(rest)
    blocks.insert(0, direct)
    raw = reduce(tables, blocks, adjoint_major)

    if further:
        def late_pass():
            total = jnp.zeros_like(raw)
            for first in range(DIRECT, ranks, DIRECT):
                chosen = late & (rank >= first) & (rank < first + DIRECT)
                kept = held_late[..., first : first + DIRECT].reshape(devices, DIRECT)
                total += reduce([table_of(kept)], [send_direct(chosen, first)], adjoint_major)
            return total

        raw = raw + lax.cond(jnp.max(notes[..., -1]) > 0, late_pass, lambda: jnp.zeros_like(raw))

    slab = (
        raw.reshape(2, NBY, NBZ, E, E, E)
        .transpose(0, 3, 1, 4, 2, 5)
        .reshape(2, E, NBY * E, NBZ * E)
    )
    summed = lax.psum(slab, "src")
    padded = with_halo(summed, (("vol", 1),), 4)
    field = smooth_axis(padded, 1)
    for axis in (2, 3):
        field = smooth_axis(pad_axis(field, axis), axis)
    return field


def solution(mesh):
    in_specs = (
        P(("src", "vol"), None, None),
        P(("src", "vol")),
        P(("src", "vol")),
        P(),
        P(),
        P("src", "vol", None, None),
    )
    out_specs = P(None, "vol", None, None)
    return jax.shard_map(local, mesh=mesh, in_specs=in_specs, out_specs=out_specs, check_vma=False)
```

```python
import functools
import math

import jax
import jax.numpy as jnp
from jax import lax
from jax.experimental import pallas as pl
from jax.experimental.pallas import tpu as pltpu
from jax.sharding import PartitionSpec as P

E = 8
NBY = 2
NBZ = 16
GROUP = 4
DIRECT = 4
SPILL = 16
PARAMS = pltpu.CompilerParams(vmem_limit_bytes=48 * 1024 * 1024)


def with_halo(cells, sides, width):
    for axis, dim in sides:
        count = lax.axis_size(axis)
        ends = count - 1
        head = lax.slice_in_dim(cells, 0, width, axis=dim)
        tail = lax.slice_in_dim(cells, cells.shape[dim] - width, cells.shape[dim], axis=dim)
        cells = jnp.concatenate(
            [
                lax.ppermute(tail, axis, [(i, (i + 1) % count) for i in range(ends)]),
                cells,
                lax.ppermute(head, axis, [((i + 1) % count, i) for i in range(ends)]),
            ],
            axis=dim,
        )
    return cells


def tap_weights():
    raw_taps = [math.exp(-(offset - 4) * (offset - 4) / 4.5) for offset in range(9)]
    tap_total = sum(raw_taps)
    return [tap_value / tap_total for tap_value in raw_taps]


def smooth_axis(padded, axis):
    weights = tap_weights()
    length = padded.shape[axis] - 8
    summed = jnp.zeros(padded.shape[:axis] + (length,) + padded.shape[axis + 1 :], jnp.float32)
    for offset in range(9):
        summed = summed + weights[offset] * lax.slice_in_dim(
            padded, offset, offset + length, axis=axis
        )
    return summed


def pad_axis(field, axis):
    widths = [(0, 0)] * field.ndim
    widths[axis] = (4, 4)
    return jnp.pad(field, widths)


def lookup(indices, table):
    hits = indices[:, None] == jnp.arange(table.shape[0], dtype=jnp.int32)[None, :]
    return jnp.sum(jnp.where(hits, table[None, :], 0), axis=1)


def place(slots, values, total):
    hits = slots[None, :] == jnp.arange(total, dtype=jnp.int32)[:, None]
    return jnp.sum(jnp.where(hits, values[None, :] + 1, 0), axis=1) - 1


def same_channel(table, row_axis, column_axis):
    table = jnp.expand_dims(table, (row_axis, column_axis))
    shape = [1] * table.ndim
    shape[row_axis] = shape[column_axis] = GROUP
    return table & jnp.eye(GROUP, dtype=bool).reshape(shape)


def route_body(table_ref, cells_ref, out_ref):
    rows = cells_ref[...].reshape(-1, cells_ref.shape[-1])
    moved = jnp.dot(table_ref[...], rows, preferred_element_type=jnp.float32)
    out_ref[...] = moved.astype(out_ref.dtype).reshape(out_ref.shape)


def route(table, cells, spec, parts):
    groups = cells.shape[0] // GROUP if cells.ndim == 3 else cells.shape[1]
    rows = table.shape[0] // parts
    width = cells.shape[-1]
    return pl.pallas_call(
        route_body,
        grid=(groups,),
        in_specs=[pl.BlockSpec(table.shape, lambda g: (0, 0)), spec],
        out_specs=pl.BlockSpec((parts, 1, rows, width), lambda g: (0, g, 0, 0)),
        out_shape=jax.ShapeDtypeStruct((parts, groups, rows, width), cells.dtype),
        compiler_params=PARAMS,
    )(table, cells)


def pack(table, forward, parts):
    slots, stored = table.shape[1:]
    table = same_channel(table, 1, 3).astype(forward.dtype)
    table = table.reshape(parts * GROUP * slots, GROUP * stored)
    spec = pl.BlockSpec((GROUP,) + forward.shape[1:], lambda g: (g, 0, 0))
    return route(table, forward, spec, parts)


def row_ids(shape, slots):
    row = lax.broadcasted_iota(jnp.int32, shape, 0)
    part, inner = row // (GROUP * slots), row % (GROUP * slots)
    return part * slots + inner % slots, inner // slots


def pick_table(wanted, row_channel, per_channel):
    column = lax.broadcasted_iota(jnp.int32, row_channel.shape, 1) // per_channel
    return jnp.where(wanted & (row_channel == column), 1.0, 0.0).astype(jnp.bfloat16)


def exchange_body(src_count, vol_count, further, *refs):
    if further:
        (slots_ref, codes_ref, notes_ref, cells_ref, direct_in, notes_in, rest_in) = refs[:7]
        (direct_out, sends, receives, own, spill_out, spill_in, codes_in, rest_out) = refs[7:15]
        (spill_sends, spill_receives, rest_sends, rest_receives) = refs[15:]
    else:
        (slots_ref, notes_ref, cells_ref, direct_in, notes_in) = refs[:5]
        (direct_out, sends, receives, own) = refs[5:]
    my_src, my_vol = lax.axis_index("src"), lax.axis_index("vol")
    devices = src_count * vol_count
    me = my_src * vol_count + my_vol
    channels, stored, width = cells_ref.shape
    groups = channels // GROUP
    mesh_ids = pl.DeviceIdType.MESH

    barrier = pltpu.get_barrier_semaphore()

    def greet(step, carry):
        peer = lax.rem(me + step, devices)
        pl.semaphore_signal(
            barrier,
            inc=1,
            device_id=(peer // vol_count, lax.rem(peer, vol_count)),
            device_id_type=mesh_ids,
        )
        return carry

    lax.fori_loop(1, devices, greet, 0)

    def pack_into(out, parts, slots, row):
        shape = (parts * GROUP * slots, GROUP * stored)
        number, channel = row_ids(shape, slots)
        holders = slots_ref[row : row + 1, :]
        holders = jnp.concatenate([holders] * GROUP, axis=1)
        table = pick_table(number == holders, channel, stored)

        def pack_group(group, carry):
            cells = cells_ref[pl.ds(group * GROUP, GROUP)].reshape(GROUP * stored, width)
            moved = jnp.dot(table, cells, preferred_element_type=jnp.float32)
            out[:, group] = moved.astype(jnp.bfloat16).reshape(parts, GROUP * slots, width)
            return carry

        lax.fori_loop(0, groups, pack_group, 0)

    def spill_copies(hop):
        plane = lax.rem(my_src + hop, src_count)
        return [
            pltpu.make_async_remote_copy(
                src_ref=source.at[plane],
                dst_ref=target.at[my_src],
                send_sem=spill_sends.at[kind, hop],
                recv_sem=spill_receives.at[kind, hop],
                device_id=(plane, my_vol),
                device_id_type=mesh_ids,
            )
            for kind, (source, target) in enumerate(
                ((codes_ref, codes_in), (spill_out, spill_in))
            )
        ]

    def direct_copies(hop, turn):
        plane = lax.rem(my_src + hop, src_count)
        column = lax.rem(my_vol + turn, vol_count)
        peer = plane * vol_count + column
        return [
            pltpu.make_async_remote_copy(
                src_ref=source.at[peer],
                dst_ref=target.at[me],
                send_sem=sends.at[kind, hop * vol_count + turn],
                recv_sem=receives.at[kind, hop * vol_count + turn],
                device_id=(plane, column),
                device_id_type=mesh_ids,
            )
            for kind, (source, target) in enumerate(
                ((notes_ref, notes_in), (direct_out, direct_in))
            )
        ]

    def rest_copy(origin, hop, turn):
        column = lax.rem(my_vol + turn, vol_count)
        return pltpu.make_async_remote_copy(
            src_ref=rest_out.at[origin, column],
            dst_ref=rest_in.at[origin * vol_count + my_vol],
            send_sem=rest_sends.at[hop, turn],
            recv_sem=rest_receives.at[hop, turn],
            device_id=(my_src, column),
            device_id_type=mesh_ids,
        )

    def each_turn(hop, act):
        def body(turn, carry):
            act(turn)
            return carry

        lax.fori_loop(1 if hop == 0 else 0, vol_count, body, 0)

    hops = sorted(range(src_count), key=lambda hop: (hop == 0, abs(2 * hop - src_count), hop))
    if further:
        pack_into(spill_out, src_count, SPILL, 1)
    pl.semaphore_wait(barrier, devices - 1)
    if further:
        for hop in hops:
            if hop:
                for copy in spill_copies(hop):
                    copy.start()
    pack_into(direct_out, devices, DIRECT, 0)
    for hop in hops:

        def begin(turn):
            for copy in direct_copies(hop, turn):
                copy.start()

        each_turn(hop, begin)
    kept = [
        pltpu.make_async_copy(direct_out.at[me], direct_in.at[me], own.at[0]),
        pltpu.make_async_copy(notes_ref.at[me], notes_in.at[me], own.at[1]),
    ]
    if further:
        for hop in sorted(range(src_count), key=lambda hop: (min(hop, src_count - hop), hop)):
            origin = lax.rem(my_src + src_count - hop, src_count)
            if hop:
                for copy in spill_copies(hop):
                    copy.wait_recv()
            codes, spill = (codes_in, spill_in) if hop else (codes_ref, spill_out)
            code = codes[origin].astype(jnp.float32)[0:1, : GROUP * SPILL].astype(jnp.int32)
            number, channel = row_ids((vol_count * GROUP * further, GROUP * SPILL), further)
            table = pick_table(number == code, channel, SPILL)

            def repack(group, carry):
                moved = jnp.dot(table, spill[origin, group], preferred_element_type=jnp.float32)
                moved = moved.astype(jnp.bfloat16)
                rest_out[origin, :, group] = moved.reshape(vol_count, GROUP * further, width)
                return carry

            lax.fori_loop(0, groups, repack, 0)
            each_turn(0, lambda turn: rest_copy(origin, hop, turn).start())
            kept.append(
                pltpu.make_async_copy(
                    rest_out.at[origin, my_vol],
                    rest_in.at[origin * vol_count + my_vol],
                    own.at[2 + hop],
                )
            )
    for copy in kept:
        copy.start()
    for copy in kept:
        copy.wait()
    if further:
        for hop in range(1, src_count):
            for copy in spill_copies(hop):
                copy.wait_send()
        for hop in range(src_count):
            origin = lax.rem(my_src + src_count - hop, src_count)
            each_turn(0, lambda turn: rest_copy(origin, hop, turn).wait())
    for hop in hops:

        def finish(turn):
            for copy in direct_copies(hop, turn):
                copy.wait()

        each_turn(hop, finish)


def exchange(slots, codes, notes, cells, src_count, vol_count, further):
    channels, _, width = cells.shape
    groups = channels // GROUP
    devices = src_count * vol_count
    kind = cells.dtype
    chunk = (groups, GROUP * DIRECT, width)
    inputs = [slots] + ([codes] if further else []) + [notes, cells]
    outputs = [(devices,) + chunk, notes.shape] + ([(devices,) + chunk] if further else [])
    dma = pltpu.SemaphoreType.DMA
    scratch = [
        pltpu.VMEM((devices,) + chunk, kind),
        dma((2, devices)),
        dma((2, devices)),
        dma((2 + src_count,)),
    ]
    if further:
        spill = pltpu.VMEM((src_count, groups, GROUP * SPILL, width), kind)
        scratch += [spill, spill, pltpu.VMEM(codes.shape, codes.dtype)]
        scratch += [pltpu.VMEM((src_count, vol_count) + chunk, kind)]
        scratch += [dma((2, src_count))] * 2 + [dma((src_count, vol_count))] * 2
    return pl.pallas_call(
        functools.partial(exchange_body, src_count, vol_count, further),
        in_specs=[pl.BlockSpec(memory_space=pltpu.VMEM)] * len(inputs),
        out_specs=[pl.BlockSpec(memory_space=pl.ANY)] * len(outputs),
        out_shape=[jax.ShapeDtypeStruct(shape, kind) for shape in outputs],
        scratch_shapes=scratch,
        compiler_params=pltpu.CompilerParams(
            collective_id=0, has_side_effects=True, vmem_limit_bytes=56 * 1024 * 1024
        ),
    )(*inputs)


def reduce_body(firsts, notes_ref, *refs):
    count = len(firsts)
    blocks, (adjoint_ref, out_ref, tables) = refs[:count], refs[count:]
    step = pl.program_id(0)
    local_tx, _, bricks, width = adjoint_ref.shape
    pairs = local_tx * bricks

    @pl.when(step == 0)
    def _():
        out_ref[...] = jnp.zeros_like(out_ref)
        notes = notes_ref[...].astype(jnp.float32)
        for at, first in enumerate(firsts):
            rows = notes[:, first : first + DIRECT]
            rows = jnp.concatenate([rows] * GROUP, axis=1).reshape(-1, pairs)
            rows = rows.T
            channel = lax.broadcasted_iota(jnp.int32, rows.shape, 1) // DIRECT % GROUP
            for group in range(GROUP):
                kept = jnp.where(channel == group, rows, 0.0).astype(tables.dtype)
                tables[at, group * pairs : (group + 1) * pairs] = kept

    summed = 0.0
    for at, block_ref in enumerate(blocks):
        rows = block_ref[...].reshape(-1, width)
        summed += jnp.dot(tables[at], rows, preferred_element_type=jnp.float32)
    summed = summed.reshape(GROUP, local_tx, bricks, width)
    for pair in range(GROUP // 2):
        total = 0.0
        for tx in range(local_tx):
            real = adjoint_ref[tx, 2 * pair].astype(jnp.float32)
            imag = adjoint_ref[tx, 2 * pair + 1].astype(jnp.float32)
            total += summed[2 * pair, tx] * real - summed[2 * pair + 1, tx] * imag
        vertical = lax.rem(step * (GROUP // 2) + pair, 3) == 2
        out_ref[0] += jnp.where(vertical, 0.0, total)
        out_ref[1] += jnp.where(vertical, total, 0.0)


def reduce(notes, firsts, blocks, adjoint):
    local_tx, channels, bricks, width = adjoint.shape
    sources = notes.shape[0]
    block = pl.BlockSpec((sources, 1) + blocks[0].shape[2:], lambda g: (0, g, 0, 0))
    table = (len(firsts), GROUP * local_tx * bricks, sources * GROUP * DIRECT)
    return pl.pallas_call(
        functools.partial(reduce_body, firsts),
        grid=(channels // GROUP,),
        in_specs=[pl.BlockSpec(notes.shape, lambda g: (0, 0, 0))]
        + [block] * len(blocks)
        + [pl.BlockSpec((local_tx, GROUP, bricks, width), lambda g: (0, g, 0, 0))],
        out_specs=pl.BlockSpec((2, bricks, width), lambda g: (0, 0, 0)),
        out_shape=jax.ShapeDtypeStruct((2, bricks, width), jnp.float32),
        scratch_shapes=[pltpu.VMEM(table, jnp.bfloat16)],
        compiler_params=PARAMS,
    )(notes, *blocks, adjoint)


def local(forward, item_tx, item_brick, tx_place, brick_place, adjoint):
    stored = forward.shape[0]
    src_count = lax.axis_size("src")
    vol_count = lax.axis_size("vol")
    devices = src_count * vol_count
    local_tx, local_bricks = adjoint.shape[:2]
    pairs = local_tx * local_bricks
    capacity = max(2, 2 * stored // devices)
    further = DIRECT if capacity > DIRECT else 0
    ranks = DIRECT + further
    assert capacity <= 2 * DIRECT
    both = ("src", "vol")
    kind = forward.dtype

    tx_at = lookup(item_tx, tx_place)
    brick_at = lookup(item_brick, brick_place)
    plane = tx_at // local_tx
    column = brick_at // local_bricks
    owner = plane * vol_count + column
    pair = tx_at % local_tx * local_bricks + brick_at % local_bricks
    positions = jnp.arange(stored, dtype=jnp.int32)
    earlier = positions[:, None] > positions[None, :]
    rank = jnp.sum((owner[:, None] == owner[None, :]) & earlier, axis=1, dtype=jnp.int32)
    spilled = rank >= DIRECT
    before = earlier & spilled[None, :] & (plane[:, None] == plane[None, :])
    spill_rank = jnp.sum(before, axis=1, dtype=jnp.int32)
    late = spilled & (spill_rank >= SPILL)

    channel_major = forward.transpose(1, 0, 2)
    adjoint_major = adjoint.transpose(0, 2, 1, 3)

    note_rank = jnp.where(late, rank + DIRECT, rank)
    listed = place(owner * 16 + note_rank, pair, devices * 16).reshape(devices, 16)
    notes = listed[:, :, None] == jnp.arange(pairs, dtype=jnp.int32)[None, None, :]
    flag_row = jnp.arange(16, dtype=jnp.int32)[None, :, None] == 15
    notes = jnp.where(flag_row, jnp.any(late), notes).astype(kind)
    direct_slot = jnp.where(spilled, -1, owner * DIRECT + rank)
    spill_slot = jnp.where(spilled & ~late, plane * SPILL + spill_rank, -1)
    slots = jnp.zeros((8, stored), jnp.int32).at[0].set(direct_slot).at[1].set(spill_slot)
    codes = None
    if further:
        codes = place(spill_slot, column * further + rank - DIRECT, src_count * SPILL)
        codes = jnp.tile(codes.reshape(src_count, 1, SPILL), (1, 16, 128 // SPILL)).astype(kind)
    moved = exchange(slots, codes, notes, channel_major, src_count, vol_count, further)
    notes = moved[1]
    firsts = (0, DIRECT) if further else (0,)
    raw = reduce(notes, firsts, [moved[0]] + list(moved[2:]), adjoint_major)

    if further:

        def late_pass():
            wanted = jnp.arange(devices * DIRECT, dtype=jnp.int32).reshape(devices, DIRECT)
            slot = jnp.where(late, owner * DIRECT + rank - DIRECT, -1)
            packed = pack(wanted[:, :, None] == slot[None, None, :], channel_major, devices)
            bricks = lax.all_to_all(packed, both, split_axis=0, concat_axis=0, tiled=True)
            return raw + reduce(notes, (2 * DIRECT,), [bricks], adjoint_major)

        raw = lax.cond(jnp.max(notes[:, 15, 0]) > 0, late_pass, lambda: raw)

    slab = (
        raw.reshape(2, NBY, NBZ, E, E, E)
        .transpose(0, 3, 1, 4, 2, 5)
        .reshape(2, E, NBY * E, NBZ * E)
    )
    summed = lax.psum(slab, "src")
    padded = with_halo(summed, (("vol", 1),), 4)
    field = smooth_axis(padded, 1)
    for axis in (2, 3):
        field = smooth_axis(pad_axis(field, axis), axis)
    return field


def solution(mesh):
    in_specs = (
        P(("src", "vol"), None, None),
        P(("src", "vol")),
        P(("src", "vol")),
        P(),
        P(),
        P("src", "vol", None, None),
    )
    out_specs = P(None, "vol", None, None)
    return jax.shard_map(local, mesh=mesh, in_specs=in_specs, out_specs=out_specs, check_vma=False)
```

```python
import functools
import math

import jax
import jax.numpy as jnp
from jax import lax
from jax.experimental import pallas as pl
from jax.experimental.pallas import tpu as pltpu
from jax.sharding import PartitionSpec as P

E = 8
NBY = 2
NBZ = 16
HALO = 4
GROUP = 4
DIRECT = 4
SPILL = 16
PARAMS = pltpu.CompilerParams(vmem_limit_bytes=48 * 1024 * 1024)


def tap_weights():
    raw_taps = [math.exp(-(offset - 4) * (offset - 4) / 4.5) for offset in range(9)]
    tap_total = sum(raw_taps)
    return [tap_value / tap_total for tap_value in raw_taps]


def lookup(indices, table):
    hits = indices[:, None] == jnp.arange(table.shape[0], dtype=jnp.int32)[None, :]
    return jnp.sum(jnp.where(hits, table[None, :], 0), axis=1)


def place(slots, values, total):
    hits = slots[None, :] == jnp.arange(total, dtype=jnp.int32)[:, None]
    return jnp.sum(jnp.where(hits, values[None, :] + 1, 0), axis=1) - 1


def same_channel(table, row_axis, column_axis):
    table = jnp.expand_dims(table, (row_axis, column_axis))
    shape = [1] * table.ndim
    shape[row_axis] = shape[column_axis] = GROUP
    return table & jnp.eye(GROUP, dtype=bool).reshape(shape)


def route_body(table_ref, cells_ref, out_ref):
    rows = cells_ref[...].reshape(-1, cells_ref.shape[-1])
    moved = jnp.dot(table_ref[...], rows, preferred_element_type=jnp.float32)
    out_ref[...] = moved.astype(out_ref.dtype).reshape(out_ref.shape)


def route(table, cells, spec, parts):
    groups = cells.shape[0] // GROUP if cells.ndim == 3 else cells.shape[1]
    rows = table.shape[0] // parts
    width = cells.shape[-1]
    return pl.pallas_call(
        route_body,
        grid=(groups,),
        in_specs=[pl.BlockSpec(table.shape, lambda g: (0, 0)), spec],
        out_specs=pl.BlockSpec((parts, 1, rows, width), lambda g: (0, g, 0, 0)),
        out_shape=jax.ShapeDtypeStruct((parts, groups, rows, width), cells.dtype),
        compiler_params=PARAMS,
    )(table, cells)


def pack(table, forward, parts):
    slots, stored = table.shape[1:]
    table = same_channel(table, 1, 3).astype(forward.dtype)
    table = table.reshape(parts * GROUP * slots, GROUP * stored)
    spec = pl.BlockSpec((GROUP,) + forward.shape[1:], lambda g: (g, 0, 0))
    return route(table, forward, spec, parts)


def row_ids(shape, slots):
    row = lax.broadcasted_iota(jnp.int32, shape, 0)
    part, inner = row // (GROUP * slots), row % (GROUP * slots)
    return part * slots + inner % slots, inner // slots


def pick_table(wanted, row_channel, per_channel):
    column = lax.broadcasted_iota(jnp.int32, row_channel.shape, 1) // per_channel
    return jnp.where(wanted & (row_channel == column), 1.0, 0.0).astype(jnp.bfloat16)


def exchange_body(src_count, vol_count, further, *refs):
    if further:
        (slots_ref, codes_ref, notes_ref, cells_ref, direct_in, notes_in, rest_in) = refs[:7]
        (direct_out, sends, receives, own, spill_out, spill_in, codes_in, rest_out) = refs[7:15]
        (spill_sends, spill_receives, rest_sends, rest_receives) = refs[15:]
    else:
        (slots_ref, notes_ref, cells_ref, direct_in, notes_in) = refs[:5]
        (direct_out, sends, receives, own) = refs[5:]
    my_src, my_vol = lax.axis_index("src"), lax.axis_index("vol")
    devices = src_count * vol_count
    me = my_src * vol_count + my_vol
    channels, stored, width = cells_ref.shape
    groups = channels // GROUP
    mesh_ids = pl.DeviceIdType.MESH

    barrier = pltpu.get_barrier_semaphore()

    def greet(step, carry):
        peer = lax.rem(me + step, devices)
        pl.semaphore_signal(
            barrier,
            inc=1,
            device_id=(peer // vol_count, lax.rem(peer, vol_count)),
            device_id_type=mesh_ids,
        )
        return carry

    lax.fori_loop(1, devices, greet, 0)

    def pack_into(out, parts, slots, row):
        shape = (parts * GROUP * slots, GROUP * stored)
        number, channel = row_ids(shape, slots)
        holders = slots_ref[row : row + 1, :]
        holders = jnp.concatenate([holders] * GROUP, axis=1)
        table = pick_table(number == holders, channel, stored)

        def pack_group(group, carry):
            cells = cells_ref[pl.ds(group * GROUP, GROUP)].reshape(GROUP * stored, width)
            moved = jnp.dot(table, cells, preferred_element_type=jnp.float32)
            out[:, group] = moved.astype(jnp.bfloat16).reshape(parts, GROUP * slots, width)
            return carry

        lax.fori_loop(0, groups, pack_group, 0)

    def spill_copies(hop):
        plane = lax.rem(my_src + hop, src_count)
        return [
            pltpu.make_async_remote_copy(
                src_ref=source.at[plane],
                dst_ref=target.at[my_src],
                send_sem=spill_sends.at[kind, hop],
                recv_sem=spill_receives.at[kind, hop],
                device_id=(plane, my_vol),
                device_id_type=mesh_ids,
            )
            for kind, (source, target) in enumerate(
                ((codes_ref, codes_in), (spill_out, spill_in))
            )
        ]

    def direct_copies(hop, turn):
        plane = lax.rem(my_src + hop, src_count)
        column = lax.rem(my_vol + turn, vol_count)
        peer = plane * vol_count + column
        return [
            pltpu.make_async_remote_copy(
                src_ref=source.at[peer],
                dst_ref=target.at[me],
                send_sem=sends.at[kind, hop * vol_count + turn],
                recv_sem=receives.at[kind, hop * vol_count + turn],
                device_id=(plane, column),
                device_id_type=mesh_ids,
            )
            for kind, (source, target) in enumerate(
                ((notes_ref, notes_in), (direct_out, direct_in))
            )
        ]

    def rest_copy(origin, hop, turn):
        column = lax.rem(my_vol + turn, vol_count)
        return pltpu.make_async_remote_copy(
            src_ref=rest_out.at[origin, column],
            dst_ref=rest_in.at[origin * vol_count + my_vol],
            send_sem=rest_sends.at[hop, turn],
            recv_sem=rest_receives.at[hop, turn],
            device_id=(my_src, column),
            device_id_type=mesh_ids,
        )

    def each_turn(hop, act):
        def body(turn, carry):
            act(turn)
            return carry

        lax.fori_loop(1 if hop == 0 else 0, vol_count, body, 0)

    hops = sorted(range(src_count), key=lambda hop: (hop == 0, abs(2 * hop - src_count), hop))
    if further:
        pack_into(spill_out, src_count, SPILL, 1)
    pl.semaphore_wait(barrier, devices - 1)
    if further:
        for hop in hops:
            if hop:
                for copy in spill_copies(hop):
                    copy.start()
    pack_into(direct_out, devices, DIRECT, 0)
    for hop in [0] + hops[:-1]:
        if further and hop == hops[0]:
            for first in hops[:-1]:
                for copy in spill_copies(first):
                    copy.wait_send()

        def begin(turn):
            for copy in direct_copies(hop, turn):
                copy.start()

        each_turn(hop, begin)
    kept = [
        pltpu.make_async_copy(direct_out.at[me], direct_in.at[me], own.at[0]),
        pltpu.make_async_copy(notes_ref.at[me], notes_in.at[me], own.at[1]),
    ]
    if further:
        for hop in sorted(range(src_count), key=lambda hop: (min(hop, src_count - hop), hop)):
            origin = lax.rem(my_src + src_count - hop, src_count)
            if hop:
                for copy in spill_copies(hop):
                    copy.wait_recv()
            codes, spill = (codes_in, spill_in) if hop else (codes_ref, spill_out)
            code = codes[origin].astype(jnp.float32)[0:1, : GROUP * SPILL].astype(jnp.int32)
            number, channel = row_ids((vol_count * GROUP * further, GROUP * SPILL), further)
            table = pick_table(number == code, channel, SPILL)

            def repack(group, carry):
                moved = jnp.dot(table, spill[origin, group], preferred_element_type=jnp.float32)
                moved = moved.astype(jnp.bfloat16)
                rest_out[origin, :, group] = moved.reshape(vol_count, GROUP * further, width)
                return carry

            lax.fori_loop(0, groups, repack, 0)
            each_turn(0, lambda turn: rest_copy(origin, hop, turn).start())
            kept.append(
                pltpu.make_async_copy(
                    rest_out.at[origin, my_vol],
                    rest_in.at[origin * vol_count + my_vol],
                    own.at[2 + hop],
                )
            )
    for copy in kept:
        copy.start()
    for copy in kept:
        copy.wait()
    if further:
        for hop in range(src_count):
            origin = lax.rem(my_src + src_count - hop, src_count)
            each_turn(0, lambda turn: rest_copy(origin, hop, turn).wait())
    for hop in hops:

        def finish(turn):
            for copy in direct_copies(hop, turn):
                copy.wait()

        each_turn(hop, finish)


def exchange(slots, codes, notes, cells, src_count, vol_count, further):
    channels, _, width = cells.shape
    groups = channels // GROUP
    devices = src_count * vol_count
    kind = cells.dtype
    chunk = (groups, GROUP * DIRECT, width)
    inputs = [slots] + ([codes] if further else []) + [notes, cells]
    outputs = [(devices,) + chunk, notes.shape] + ([(devices,) + chunk] if further else [])
    dma = pltpu.SemaphoreType.DMA
    scratch = [
        pltpu.VMEM((devices,) + chunk, kind),
        dma((2, devices)),
        dma((2, devices)),
        dma((2 + src_count,)),
    ]
    if further:
        spill = pltpu.VMEM((src_count, groups, GROUP * SPILL, width), kind)
        scratch += [spill, spill, pltpu.VMEM(codes.shape, codes.dtype)]
        scratch += [pltpu.VMEM((src_count, vol_count) + chunk, kind)]
        scratch += [dma((2, src_count))] * 2 + [dma((src_count, vol_count))] * 2
    return pl.pallas_call(
        functools.partial(exchange_body, src_count, vol_count, further),
        in_specs=[pl.BlockSpec(memory_space=pltpu.VMEM)] * len(inputs),
        out_specs=[pl.BlockSpec(memory_space=pl.ANY)] * len(outputs),
        out_shape=[jax.ShapeDtypeStruct(shape, kind) for shape in outputs],
        scratch_shapes=scratch,
        compiler_params=pltpu.CompilerParams(
            collective_id=0, has_side_effects=True, vmem_limit_bytes=56 * 1024 * 1024
        ),
    )(*inputs)


def reduce_body(firsts, notes_ref, *refs):
    count = len(firsts)
    blocks, (adjoint_ref, out_ref, tables) = refs[:count], refs[count:]
    step = pl.program_id(0)
    local_tx, _, bricks, width = adjoint_ref.shape
    pairs = local_tx * bricks

    @pl.when(step == 0)
    def _():
        out_ref[...] = jnp.zeros_like(out_ref)
        notes = notes_ref[...].astype(jnp.float32)
        for at, first in enumerate(firsts):
            rows = notes[:, first : first + DIRECT]
            rows = jnp.concatenate([rows] * GROUP, axis=1).reshape(-1, pairs)
            rows = rows.T
            channel = lax.broadcasted_iota(jnp.int32, rows.shape, 1) // DIRECT % GROUP
            for group in range(GROUP):
                kept = jnp.where(channel == group, rows, 0.0).astype(tables.dtype)
                tables[at, group * pairs : (group + 1) * pairs] = kept

    summed = 0.0
    for at, block_ref in enumerate(blocks):
        rows = block_ref[...].reshape(-1, width)
        summed += jnp.dot(tables[at], rows, preferred_element_type=jnp.float32)
    summed = summed.reshape(GROUP, local_tx, bricks, width)
    for pair in range(GROUP // 2):
        total = 0.0
        for tx in range(local_tx):
            real = adjoint_ref[tx, 2 * pair].astype(jnp.float32)
            imag = adjoint_ref[tx, 2 * pair + 1].astype(jnp.float32)
            total += summed[2 * pair, tx] * real - summed[2 * pair + 1, tx] * imag
        vertical = lax.rem(step * (GROUP // 2) + pair, 3) == 2
        out_ref[0] += jnp.where(vertical, 0.0, total)
        out_ref[1] += jnp.where(vertical, total, 0.0)


def reduce(notes, firsts, blocks, adjoint):
    local_tx, channels, bricks, width = adjoint.shape
    sources = notes.shape[0]
    block = pl.BlockSpec((sources, 1) + blocks[0].shape[2:], lambda g: (0, g, 0, 0))
    table = (len(firsts), GROUP * local_tx * bricks, sources * GROUP * DIRECT)
    return pl.pallas_call(
        functools.partial(reduce_body, firsts),
        grid=(channels // GROUP,),
        in_specs=[pl.BlockSpec(notes.shape, lambda g: (0, 0, 0))]
        + [block] * len(blocks)
        + [pl.BlockSpec((local_tx, GROUP, bricks, width), lambda g: (0, g, 0, 0))],
        out_specs=pl.BlockSpec((2, bricks, width), lambda g: (0, 0, 0)),
        out_shape=jax.ShapeDtypeStruct((2, bricks, width), jnp.float32),
        scratch_shapes=[pltpu.VMEM(table, jnp.bfloat16)],
        compiler_params=PARAMS,
    )(notes, *blocks, adjoint)


def smooth_body(src_count, vol_count, slab_ref, out_ref, mid, low, high, sends, receives):
    my_src, my_vol = lax.axis_index("src"), lax.axis_index("vol")
    length, _, rows, columns = slab_ref.shape
    mesh_ids = pl.DeviceIdType.MESH
    has_low, has_high = my_vol > 0, my_vol < vol_count - 1

    def copies(hop, side):
        plane = lax.rem(my_src + hop, src_count)
        source, target = {
            0: (slab_ref, mid),
            -1: (slab_ref.at[pl.ds(0, HALO)], high),
            1: (slab_ref.at[pl.ds(length - HALO, HALO)], low),
        }[side]
        return pltpu.make_async_remote_copy(
            src_ref=source,
            dst_ref=target.at[my_src],
            send_sem=sends.at[side + 1, hop],
            recv_sem=receives.at[side + 1, hop],
            device_id=(plane, lax.rem(my_vol + side + vol_count, vol_count)),
            device_id_type=mesh_ids,
        )

    barrier = pltpu.get_barrier_semaphore()

    def greet(side):
        for hop in range(0 if side else 1, src_count):
            pl.semaphore_signal(
                barrier,
                inc=1,
                device_id=(lax.rem(my_src + hop, src_count), my_vol + side),
                device_id_type=mesh_ids,
            )

    greet(0)
    pl.when(has_low)(lambda: greet(-1))
    pl.when(has_high)(lambda: greet(1))
    sides = jnp.where(has_low, 1, 0) + jnp.where(has_high, 1, 0)
    pl.semaphore_wait(barrier, src_count - 1 + src_count * sides)

    def start(side):
        for hop in range(0 if side else 1, src_count):
            copies(hop, side).start()

    start(0)
    pl.when(has_low)(lambda: start(-1))
    pl.when(has_high)(lambda: start(1))
    mid[my_src] = slab_ref[...]

    @pl.when(jnp.logical_not(has_low))
    def _():
        low[...] = jnp.zeros_like(low)

    @pl.when(jnp.logical_not(has_high))
    def _():
        high[...] = jnp.zeros_like(high)

    def finish(side):
        for hop in range(0 if side else 1, src_count):
            copies(hop, side).wait_send()
            copies(hop, -side).wait_recv()

    finish(0)
    pl.when(has_low)(lambda: finish(-1))
    pl.when(has_high)(lambda: finish(1))

    weights = tap_weights()
    padded = jnp.concatenate(
        [sum(part[src] for src in range(src_count)) for part in (low, mid, high)], axis=0
    )
    field = sum(weights[at] * padded[at : at + length] for at in range(2 * HALO + 1))
    edge = jnp.zeros((length, 2, HALO, columns), jnp.float32)
    padded = jnp.concatenate([edge, field, edge], axis=2)
    field = sum(weights[at] * padded[:, :, at : at + rows] for at in range(2 * HALO + 1))
    offset = lax.broadcasted_iota(jnp.int32, (columns, columns), 0)
    offset = offset - lax.broadcasted_iota(jnp.int32, (columns, columns), 1)
    taps = sum(
        jnp.where(offset == at - HALO, weights[at], 0.0) for at in range(2 * HALO + 1)
    )
    field = jnp.dot(
        field.reshape(-1, columns),
        taps,
        precision=lax.Precision.HIGHEST,
        preferred_element_type=jnp.float32,
    ).reshape(length, 2, rows, columns)
    for at in range(length):
        out_ref[:, at] = field[at]


def smooth(slab, src_count, vol_count):
    length, kinds, rows, columns = slab.shape
    halo = pltpu.VMEM((src_count, HALO, kinds, rows, columns), jnp.float32)
    return pl.pallas_call(
        functools.partial(smooth_body, src_count, vol_count),
        in_specs=[pl.BlockSpec(memory_space=pltpu.VMEM)],
        out_specs=pl.BlockSpec(memory_space=pltpu.VMEM),
        out_shape=jax.ShapeDtypeStruct((kinds, length, rows, columns), jnp.float32),
        scratch_shapes=[
            pltpu.VMEM((src_count,) + slab.shape, jnp.float32),
            halo,
            halo,
            pltpu.SemaphoreType.DMA((3, src_count)),
            pltpu.SemaphoreType.DMA((3, src_count)),
        ],
        compiler_params=pltpu.CompilerParams(
            collective_id=1, has_side_effects=True, vmem_limit_bytes=32 * 1024 * 1024
        ),
    )(slab)


def local(forward, item_tx, item_brick, tx_place, brick_place, adjoint):
    stored = forward.shape[0]
    src_count = lax.axis_size("src")
    vol_count = lax.axis_size("vol")
    devices = src_count * vol_count
    local_tx, local_bricks = adjoint.shape[:2]
    pairs = local_tx * local_bricks
    capacity = max(2, 2 * stored // devices)
    further = DIRECT if capacity > DIRECT else 0
    ranks = DIRECT + further
    assert capacity <= 2 * DIRECT
    both = ("src", "vol")
    kind = forward.dtype

    tx_at = lookup(item_tx, tx_place)
    brick_at = lookup(item_brick, brick_place)
    plane = tx_at // local_tx
    column = brick_at // local_bricks
    owner = plane * vol_count + column
    pair = tx_at % local_tx * local_bricks + brick_at % local_bricks
    positions = jnp.arange(stored, dtype=jnp.int32)
    earlier = positions[:, None] > positions[None, :]
    rank = jnp.sum((owner[:, None] == owner[None, :]) & earlier, axis=1, dtype=jnp.int32)
    spilled = rank >= DIRECT
    before = earlier & spilled[None, :] & (plane[:, None] == plane[None, :])
    spill_rank = jnp.sum(before, axis=1, dtype=jnp.int32)
    late = spilled & (spill_rank >= SPILL)

    channel_major = forward.transpose(1, 0, 2)
    adjoint_major = adjoint.transpose(0, 2, 1, 3)

    note_rank = jnp.where(late, rank + DIRECT, rank)
    listed = place(owner * 16 + note_rank, pair, devices * 16).reshape(devices, 16)
    notes = listed[:, :, None] == jnp.arange(pairs, dtype=jnp.int32)[None, None, :]
    flag_row = jnp.arange(16, dtype=jnp.int32)[None, :, None] == 15
    notes = jnp.where(flag_row, jnp.any(late), notes).astype(kind)
    direct_slot = jnp.where(spilled, -1, owner * DIRECT + rank)
    spill_slot = jnp.where(spilled & ~late, plane * SPILL + spill_rank, -1)
    slots = jnp.zeros((8, stored), jnp.int32).at[0].set(direct_slot).at[1].set(spill_slot)
    codes = None
    if further:
        codes = place(spill_slot, column * further + rank - DIRECT, src_count * SPILL)
        codes = jnp.tile(codes.reshape(src_count, 1, SPILL), (1, 16, 128 // SPILL)).astype(kind)
    moved = exchange(slots, codes, notes, channel_major, src_count, vol_count, further)
    notes = moved[1]
    firsts = (0, DIRECT) if further else (0,)
    raw = reduce(notes, firsts, [moved[0]] + list(moved[2:]), adjoint_major)

    if further:

        def late_pass():
            wanted = jnp.arange(devices * DIRECT, dtype=jnp.int32).reshape(devices, DIRECT)
            slot = jnp.where(late, owner * DIRECT + rank - DIRECT, -1)
            packed = pack(wanted[:, :, None] == slot[None, None, :], channel_major, devices)
            bricks = lax.all_to_all(packed, both, split_axis=0, concat_axis=0, tiled=True)
            return raw + reduce(notes, (2 * DIRECT,), [bricks], adjoint_major)

        raw = lax.cond(jnp.max(notes[:, 15, 0]) > 0, late_pass, lambda: raw)

    slab = raw.reshape(2, NBY, NBZ, E, E, E).transpose(3, 0, 1, 4, 2, 5)
    return smooth(slab.reshape(E, 2, NBY * E, NBZ * E), src_count, vol_count)


def solution(mesh):
    in_specs = (
        P(("src", "vol"), None, None),
        P(("src", "vol")),
        P(("src", "vol")),
        P(),
        P(),
        P("src", "vol", None, None),
    )
    out_specs = P(None, "vol", None, None)
    return jax.shard_map(local, mesh=mesh, in_specs=in_specs, out_specs=out_specs, check_vma=False)
```

```python
import functools
import math

import jax
import jax.numpy as jnp
from jax import lax
from jax.experimental import pallas as pl
from jax.experimental.pallas import tpu as pltpu
from jax.sharding import PartitionSpec as P

E = 8
NBY = 2
NBZ = 16
HALO = 4
GROUP = 4
DIRECT = 4
SPILL = 16
PARAMS = pltpu.CompilerParams(vmem_limit_bytes=48 * 1024 * 1024)


def tap_weights():
    raw_taps = [math.exp(-(offset - 4) * (offset - 4) / 4.5) for offset in range(9)]
    tap_total = sum(raw_taps)
    return [tap_value / tap_total for tap_value in raw_taps]


def lookup(indices, table):
    hits = indices[:, None] == jnp.arange(table.shape[0], dtype=jnp.int32)[None, :]
    return jnp.sum(jnp.where(hits, table[None, :], 0), axis=1)


def place(slots, values, total):
    hits = slots[None, :] == jnp.arange(total, dtype=jnp.int32)[:, None]
    return jnp.sum(jnp.where(hits, values[None, :] + 1, 0), axis=1) - 1


def same_channel(table, row_axis, column_axis):
    table = jnp.expand_dims(table, (row_axis, column_axis))
    shape = [1] * table.ndim
    shape[row_axis] = shape[column_axis] = GROUP
    return table & jnp.eye(GROUP, dtype=bool).reshape(shape)


def route_body(table_ref, cells_ref, out_ref):
    rows = cells_ref[...].reshape(-1, cells_ref.shape[-1])
    moved = jnp.dot(table_ref[...], rows, preferred_element_type=jnp.float32)
    out_ref[...] = moved.astype(out_ref.dtype).reshape(out_ref.shape)


def route(table, cells, spec, parts):
    groups = cells.shape[0] // GROUP if cells.ndim == 3 else cells.shape[1]
    rows = table.shape[0] // parts
    width = cells.shape[-1]
    return pl.pallas_call(
        route_body,
        grid=(groups,),
        in_specs=[pl.BlockSpec(table.shape, lambda g: (0, 0)), spec],
        out_specs=pl.BlockSpec((parts, 1, rows, width), lambda g: (0, g, 0, 0)),
        out_shape=jax.ShapeDtypeStruct((parts, groups, rows, width), cells.dtype),
        compiler_params=PARAMS,
    )(table, cells)


def pack(table, forward, parts):
    slots, stored = table.shape[1:]
    table = same_channel(table, 1, 3).astype(forward.dtype)
    table = table.reshape(parts * GROUP * slots, GROUP * stored)
    spec = pl.BlockSpec((GROUP,) + forward.shape[1:], lambda g: (g, 0, 0))
    return route(table, forward, spec, parts)


def row_ids(shape, slots):
    row = lax.broadcasted_iota(jnp.int32, shape, 0)
    part, inner = row // (GROUP * slots), row % (GROUP * slots)
    return part * slots + inner % slots, inner // slots


def pick_table(wanted, row_channel, per_channel):
    column = lax.broadcasted_iota(jnp.int32, row_channel.shape, 1) // per_channel
    return jnp.where(wanted & (row_channel == column), 1.0, 0.0).astype(jnp.bfloat16)


def exchange_body(src_count, vol_count, further, *refs):
    if further:
        (slots_ref, codes_ref, notes_ref, cells_ref, direct_in, notes_in, rest_in) = refs[:7]
        (direct_out, sends, receives, own, spill_out, spill_in, codes_in, rest_out) = refs[7:15]
        (spill_sends, spill_receives, rest_sends, rest_receives) = refs[15:]
    else:
        (slots_ref, notes_ref, cells_ref, direct_in, notes_in) = refs[:5]
        (direct_out, sends, receives, own) = refs[5:]
    my_src, my_vol = lax.axis_index("src"), lax.axis_index("vol")
    devices = src_count * vol_count
    me = my_src * vol_count + my_vol
    channels, stored, width = cells_ref.shape
    groups = channels // GROUP
    mesh_ids = pl.DeviceIdType.MESH

    barrier = pltpu.get_barrier_semaphore()

    def greet(step, carry):
        peer = lax.rem(me + step, devices)
        pl.semaphore_signal(
            barrier,
            inc=1,
            device_id=(peer // vol_count, lax.rem(peer, vol_count)),
            device_id_type=mesh_ids,
        )
        return carry

    lax.fori_loop(1, devices, greet, 0)

    def pack_into(out, parts, slots, row):
        shape = (parts * GROUP * slots, GROUP * stored)
        number, channel = row_ids(shape, slots)
        holders = slots_ref[row : row + 1, :]
        holders = jnp.concatenate([holders] * GROUP, axis=1)
        table = pick_table(number == holders, channel, stored)

        def pack_group(group, carry):
            cells = cells_ref[pl.ds(group * GROUP, GROUP)].reshape(GROUP * stored, width)
            moved = jnp.dot(table, cells, preferred_element_type=jnp.float32)
            out[:, group] = moved.astype(jnp.bfloat16).reshape(parts, GROUP * slots, width)
            return carry

        lax.fori_loop(0, groups, pack_group, 0)

    def spill_copies(hop):
        plane = lax.rem(my_src + hop, src_count)
        return [
            pltpu.make_async_remote_copy(
                src_ref=source.at[plane],
                dst_ref=target.at[my_src],
                send_sem=spill_sends.at[kind, hop],
                recv_sem=spill_receives.at[kind, hop],
                device_id=(plane, my_vol),
                device_id_type=mesh_ids,
            )
            for kind, (source, target) in enumerate(
                ((codes_ref, codes_in), (spill_out, spill_in))
            )
        ]

    def direct_copies(hop, turn):
        plane = lax.rem(my_src + hop, src_count)
        column = lax.rem(my_vol + turn, vol_count)
        peer = plane * vol_count + column
        return [
            pltpu.make_async_remote_copy(
                src_ref=source.at[peer],
                dst_ref=target.at[me],
                send_sem=sends.at[kind, hop * vol_count + turn],
                recv_sem=receives.at[kind, hop * vol_count + turn],
                device_id=(plane, column),
                device_id_type=mesh_ids,
            )
            for kind, (source, target) in enumerate(
                ((notes_ref, notes_in), (direct_out, direct_in))
            )
        ]

    def rest_copy(origin, hop, turn):
        column = lax.rem(my_vol + turn, vol_count)
        return pltpu.make_async_remote_copy(
            src_ref=rest_out.at[origin, column],
            dst_ref=rest_in.at[origin * vol_count + my_vol],
            send_sem=rest_sends.at[hop, turn],
            recv_sem=rest_receives.at[hop, turn],
            device_id=(my_src, column),
            device_id_type=mesh_ids,
        )

    def each_turn(hop, act):
        def body(turn, carry):
            act(turn)
            return carry

        lax.fori_loop(1 if hop == 0 else 0, vol_count, body, 0)

    hops = sorted(range(src_count), key=lambda hop: (hop == 0, abs(2 * hop - src_count), hop))
    if further:
        pack_into(spill_out, src_count, SPILL, 1)
    pl.semaphore_wait(barrier, devices - 1)
    if further:
        for hop in hops:
            if hop:
                for copy in spill_copies(hop):
                    copy.start()
    pack_into(direct_out, devices, DIRECT, 0)
    kept = [
        pltpu.make_async_copy(direct_out.at[me], direct_in.at[me], own.at[0]),
        pltpu.make_async_copy(notes_ref.at[me], notes_in.at[me], own.at[1]),
    ]

    def send_turns(first, last):
        def body(turn, carry):
            for hop in hops:
                for copy in direct_copies(hop, turn):
                    copy.start()
            return carry

        if first == 0:
            for hop in hops[:-1]:
                for copy in direct_copies(hop, 0):
                    copy.start()
        lax.fori_loop(max(first, 1), last, body, 0)

    def send_rest(hop):
        origin = lax.rem(my_src + src_count - hop, src_count)
        if hop:
            for copy in spill_copies(hop):
                copy.wait_recv()
        codes, spill = (codes_in, spill_in) if hop else (codes_ref, spill_out)
        code = codes[origin].astype(jnp.float32)[0:1, : GROUP * SPILL].astype(jnp.int32)
        number, channel = row_ids((vol_count * GROUP * further, GROUP * SPILL), further)
        table = pick_table(number == code, channel, SPILL)

        def repack(group, carry):
            moved = jnp.dot(table, spill[origin, group], preferred_element_type=jnp.float32)
            moved = moved.astype(jnp.bfloat16)
            rest_out[origin, :, group] = moved.reshape(vol_count, GROUP * further, width)
            return carry

        lax.fori_loop(0, groups, repack, 0)
        each_turn(0, lambda turn: rest_copy(origin, hop, turn).start())
        kept.append(
            pltpu.make_async_copy(
                rest_out.at[origin, my_vol],
                rest_in.at[origin * vol_count + my_vol],
                own.at[2 + hop],
            )
        )

    turn = vol_count * 5 // 8 if further else vol_count
    if further:
        send_rest(0)
    send_turns(0, turn)
    if further:
        for hop in sorted(range(1, src_count), key=lambda hop: (min(hop, src_count - hop), hop)):
            send_rest(hop)
            if turn < vol_count:
                send_turns(turn, turn + 1)
                turn += 1
    if turn < vol_count:
        send_turns(turn, vol_count)
    for copy in kept:
        copy.start()
    for copy in kept:
        copy.wait()
    if further:
        for hop in range(1, src_count):
            for copy in spill_copies(hop):
                copy.wait_send()
        for hop in range(src_count):
            origin = lax.rem(my_src + src_count - hop, src_count)
            each_turn(0, lambda turn: rest_copy(origin, hop, turn).wait())
    for hop in hops:

        def finish(turn):
            for copy in direct_copies(hop, turn):
                copy.wait()

        each_turn(hop, finish)


def exchange(slots, codes, notes, cells, src_count, vol_count, further):
    channels, _, width = cells.shape
    groups = channels // GROUP
    devices = src_count * vol_count
    kind = cells.dtype
    chunk = (groups, GROUP * DIRECT, width)
    inputs = [slots] + ([codes] if further else []) + [notes, cells]
    outputs = [(devices,) + chunk, notes.shape] + ([(devices,) + chunk] if further else [])
    dma = pltpu.SemaphoreType.DMA
    scratch = [
        pltpu.VMEM((devices,) + chunk, kind),
        dma((2, devices)),
        dma((2, devices)),
        dma((2 + src_count,)),
    ]
    if further:
        spill = pltpu.VMEM((src_count, groups, GROUP * SPILL, width), kind)
        scratch += [spill, spill, pltpu.VMEM(codes.shape, codes.dtype)]
        scratch += [pltpu.VMEM((src_count, vol_count) + chunk, kind)]
        scratch += [dma((2, src_count))] * 2 + [dma((src_count, vol_count))] * 2
    return pl.pallas_call(
        functools.partial(exchange_body, src_count, vol_count, further),
        in_specs=[pl.BlockSpec(memory_space=pltpu.VMEM)] * len(inputs),
        out_specs=[pl.BlockSpec(memory_space=pl.ANY)] * len(outputs),
        out_shape=[jax.ShapeDtypeStruct(shape, kind) for shape in outputs],
        scratch_shapes=scratch,
        compiler_params=pltpu.CompilerParams(
            collective_id=0, has_side_effects=True, vmem_limit_bytes=56 * 1024 * 1024
        ),
    )(*inputs)


def reduce_body(firsts, notes_ref, *refs):
    count = len(firsts)
    blocks, (adjoint_ref, out_ref, tables) = refs[:count], refs[count:]
    step = pl.program_id(0)
    local_tx, _, bricks, width = adjoint_ref.shape
    pairs = local_tx * bricks

    @pl.when(step == 0)
    def _():
        out_ref[...] = jnp.zeros_like(out_ref)
        notes = notes_ref[...].astype(jnp.float32)
        for at, first in enumerate(firsts):
            rows = notes[:, first : first + DIRECT]
            rows = jnp.concatenate([rows] * GROUP, axis=1).reshape(-1, pairs)
            rows = rows.T
            channel = lax.broadcasted_iota(jnp.int32, rows.shape, 1) // DIRECT % GROUP
            for group in range(GROUP):
                kept = jnp.where(channel == group, rows, 0.0).astype(tables.dtype)
                tables[at, group * pairs : (group + 1) * pairs] = kept

    summed = 0.0
    for at, block_ref in enumerate(blocks):
        rows = block_ref[...].reshape(-1, width)
        summed += jnp.dot(tables[at], rows, preferred_element_type=jnp.float32)
    summed = summed.reshape(GROUP, local_tx, bricks, width)
    for pair in range(GROUP // 2):
        total = 0.0
        for tx in range(local_tx):
            real = adjoint_ref[tx, 2 * pair].astype(jnp.float32)
            imag = adjoint_ref[tx, 2 * pair + 1].astype(jnp.float32)
            total += summed[2 * pair, tx] * real - summed[2 * pair + 1, tx] * imag
        vertical = lax.rem(step * (GROUP // 2) + pair, 3) == 2
        out_ref[0] += jnp.where(vertical, 0.0, total)
        out_ref[1] += jnp.where(vertical, total, 0.0)


def reduce(notes, firsts, blocks, adjoint):
    local_tx, channels, bricks, width = adjoint.shape
    sources = notes.shape[0]
    block = pl.BlockSpec((sources, 1) + blocks[0].shape[2:], lambda g: (0, g, 0, 0))
    table = (len(firsts), GROUP * local_tx * bricks, sources * GROUP * DIRECT)
    return pl.pallas_call(
        functools.partial(reduce_body, firsts),
        grid=(channels // GROUP,),
        in_specs=[pl.BlockSpec(notes.shape, lambda g: (0, 0, 0))]
        + [block] * len(blocks)
        + [pl.BlockSpec((local_tx, GROUP, bricks, width), lambda g: (0, g, 0, 0))],
        out_specs=pl.BlockSpec((2, bricks, width), lambda g: (0, 0, 0)),
        out_shape=jax.ShapeDtypeStruct((2, bricks, width), jnp.float32),
        scratch_shapes=[pltpu.VMEM(table, jnp.bfloat16)],
        compiler_params=PARAMS,
    )(notes, *blocks, adjoint)


def smooth_body(src_count, vol_count, slab_ref, out_ref, mid, low, high, done, sends, receives):
    my_src, my_vol = lax.axis_index("src"), lax.axis_index("vol")
    _, length, part_rows, columns = slab_ref.shape
    kinds, _, rows, _ = out_ref.shape
    mesh_ids = pl.DeviceIdType.MESH
    has_low, has_high = my_vol > 0, my_vol < vol_count - 1
    gather = 3

    def copies(hop, side):
        plane = lax.rem(my_src + hop, src_count)
        source, target = {
            0: (slab_ref.at[plane], mid),
            -1: (slab_ref.at[plane, pl.ds(0, HALO)], high),
            1: (slab_ref.at[plane, pl.ds(length - HALO, HALO)], low),
        }[side]
        return pltpu.make_async_remote_copy(
            src_ref=source,
            dst_ref=target.at[my_src],
            send_sem=sends.at[side + 1, hop],
            recv_sem=receives.at[side + 1, hop],
            device_id=(plane, lax.rem(my_vol + side + vol_count, vol_count)),
            device_id_type=mesh_ids,
        )

    def gather_copy(hop):
        return pltpu.make_async_remote_copy(
            src_ref=done.at[my_src],
            dst_ref=done.at[my_src],
            send_sem=sends.at[gather, hop],
            recv_sem=receives.at[gather, hop],
            device_id=(lax.rem(my_src + hop, src_count), my_vol),
            device_id_type=mesh_ids,
        )

    barrier = pltpu.get_barrier_semaphore()

    def greet(side):
        for hop in range(0 if side else 1, src_count):
            pl.semaphore_signal(
                barrier,
                inc=1,
                device_id=(lax.rem(my_src + hop, src_count), my_vol + side),
                device_id_type=mesh_ids,
            )

    greet(0)
    pl.when(has_low)(lambda: greet(-1))
    pl.when(has_high)(lambda: greet(1))
    sides = jnp.where(has_low, 1, 0) + jnp.where(has_high, 1, 0)
    pl.semaphore_wait(barrier, src_count - 1 + src_count * sides)

    def start(side):
        for hop in range(0 if side else 1, src_count):
            copies(hop, side).start()

    start(0)
    pl.when(has_low)(lambda: start(-1))
    pl.when(has_high)(lambda: start(1))
    mid[my_src] = slab_ref[my_src]

    @pl.when(jnp.logical_not(has_low))
    def _():
        low[...] = jnp.zeros_like(low)

    @pl.when(jnp.logical_not(has_high))
    def _():
        high[...] = jnp.zeros_like(high)

    weights = tap_weights()
    offset = lax.broadcasted_iota(jnp.int32, (columns, columns), 0)
    offset = offset - lax.broadcasted_iota(jnp.int32, (columns, columns), 1)
    taps = sum(
        jnp.where(offset == at - HALO, weights[at], 0.0) for at in range(2 * HALO + 1)
    )

    def arrive(side):
        for hop in range(0 if side else 1, src_count):
            copies(hop, -side).wait_recv()

    arrive(0)
    pl.when(has_low)(lambda: arrive(-1))
    pl.when(has_high)(lambda: arrive(1))
    padded = jnp.concatenate(
        [sum(part[src] for src in range(src_count)) for part in (low, mid, high)], axis=0
    )
    field = sum(weights[at] * padded[at : at + length] for at in range(2 * HALO + 1))
    field = jnp.dot(
        field.reshape(-1, columns),
        taps,
        precision=lax.Precision.HIGHEST,
        preferred_element_type=jnp.float32,
    )
    done[my_src] = field.reshape(length, part_rows, columns)
    for hop in range(1, src_count):
        gather_copy(hop).start()

    def leave(side):
        for hop in range(0 if side else 1, src_count):
            copies(hop, side).wait_send()

    leave(0)
    pl.when(has_low)(lambda: leave(-1))
    pl.when(has_high)(lambda: leave(1))
    for hop in range(1, src_count):
        gather_copy(hop).wait()
    edge = jnp.zeros((length, HALO, columns), jnp.float32)
    share = src_count // kinds
    for kind in range(kinds):
        parts = [done[kind * share + at] for at in range(share)]
        padded = jnp.concatenate([edge] + parts + [edge], axis=1)
        out_ref[kind] = sum(weights[at] * padded[:, at : at + rows] for at in range(2 * HALO + 1))


def smooth(slab, src_count, vol_count):
    length, kinds, rows, columns = slab.shape
    part = (length, kinds * rows // src_count, columns)
    slab = slab.reshape(length, src_count, part[1], columns).swapaxes(0, 1)
    whole = pltpu.VMEM((src_count,) + part, jnp.float32)
    halo = pltpu.VMEM((src_count, HALO) + part[1:], jnp.float32)
    return pl.pallas_call(
        functools.partial(smooth_body, src_count, vol_count),
        in_specs=[pl.BlockSpec(memory_space=pltpu.VMEM)],
        out_specs=pl.BlockSpec(memory_space=pltpu.VMEM),
        out_shape=jax.ShapeDtypeStruct((kinds, length, rows, columns), jnp.float32),
        scratch_shapes=[
            whole,
            halo,
            halo,
            whole,
            pltpu.SemaphoreType.DMA((4, src_count)),
            pltpu.SemaphoreType.DMA((4, src_count)),
        ],
        compiler_params=pltpu.CompilerParams(
            collective_id=1, has_side_effects=True, vmem_limit_bytes=32 * 1024 * 1024
        ),
    )(slab)


def local(forward, item_tx, item_brick, tx_place, brick_place, adjoint):
    stored = forward.shape[0]
    src_count = lax.axis_size("src")
    vol_count = lax.axis_size("vol")
    devices = src_count * vol_count
    local_tx, local_bricks = adjoint.shape[:2]
    pairs = local_tx * local_bricks
    capacity = max(2, 2 * stored // devices)
    further = DIRECT if capacity > DIRECT else 0
    ranks = DIRECT + further
    assert capacity <= 2 * DIRECT
    both = ("src", "vol")
    kind = forward.dtype

    tx_at = lookup(item_tx, tx_place)
    brick_at = lookup(item_brick, brick_place)
    plane = tx_at // local_tx
    column = brick_at // local_bricks
    owner = plane * vol_count + column
    pair = tx_at % local_tx * local_bricks + brick_at % local_bricks
    positions = jnp.arange(stored, dtype=jnp.int32)
    earlier = positions[:, None] > positions[None, :]
    rank = jnp.sum((owner[:, None] == owner[None, :]) & earlier, axis=1, dtype=jnp.int32)
    spilled = rank >= DIRECT
    before = earlier & spilled[None, :] & (plane[:, None] == plane[None, :])
    spill_rank = jnp.sum(before, axis=1, dtype=jnp.int32)
    late = spilled & (spill_rank >= SPILL)

    channel_major = forward.transpose(1, 0, 2)
    adjoint_major = adjoint.transpose(0, 2, 1, 3)

    note_rank = jnp.where(late, rank + DIRECT, rank)
    listed = place(owner * 16 + note_rank, pair, devices * 16).reshape(devices, 16)
    notes = listed[:, :, None] == jnp.arange(pairs, dtype=jnp.int32)[None, None, :]
    flag_row = jnp.arange(16, dtype=jnp.int32)[None, :, None] == 15
    notes = jnp.where(flag_row, jnp.any(late), notes).astype(kind)
    direct_slot = jnp.where(spilled, -1, owner * DIRECT + rank)
    spill_slot = jnp.where(spilled & ~late, plane * SPILL + spill_rank, -1)
    slots = jnp.zeros((8, stored), jnp.int32).at[0].set(direct_slot).at[1].set(spill_slot)
    codes = None
    if further:
        codes = place(spill_slot, column * further + rank - DIRECT, src_count * SPILL)
        codes = jnp.tile(codes.reshape(src_count, 1, SPILL), (1, 16, 128 // SPILL)).astype(kind)
    moved = exchange(slots, codes, notes, channel_major, src_count, vol_count, further)
    notes = moved[1]
    firsts = (0, DIRECT) if further else (0,)
    raw = reduce(notes, firsts, [moved[0]] + list(moved[2:]), adjoint_major)

    if further:

        def late_pass():
            wanted = jnp.arange(devices * DIRECT, dtype=jnp.int32).reshape(devices, DIRECT)
            slot = jnp.where(late, owner * DIRECT + rank - DIRECT, -1)
            packed = pack(wanted[:, :, None] == slot[None, None, :], channel_major, devices)
            bricks = lax.all_to_all(packed, both, split_axis=0, concat_axis=0, tiled=True)
            return raw + reduce(notes, (2 * DIRECT,), [bricks], adjoint_major)

        raw = lax.cond(jnp.max(notes[:, 15, 0]) > 0, late_pass, lambda: raw)

    slab = raw.reshape(2, NBY, NBZ, E, E, E).transpose(3, 0, 1, 4, 2, 5)
    return smooth(slab.reshape(E, 2, NBY * E, NBZ * E), src_count, vol_count)


def solution(mesh):
    in_specs = (
        P(("src", "vol"), None, None),
        P(("src", "vol")),
        P(("src", "vol")),
        P(),
        P(),
        P("src", "vol", None, None),
    )
    out_specs = P(None, "vol", None, None)
    return jax.shard_map(local, mesh=mesh, in_specs=in_specs, out_specs=out_specs, check_vma=False)
```

```python
import functools
import math

import jax
import jax.numpy as jnp
from jax import lax
from jax.experimental import pallas as pl
from jax.experimental.pallas import tpu as pltpu
from jax.sharding import PartitionSpec as P

E = 8
NBY = 2
NBZ = 16
HALO = 4
GROUP = 4
DIRECT = 4
SPILL = 16
POOL = 20
PARAMS = pltpu.CompilerParams(vmem_limit_bytes=48 * 1024 * 1024)


def tap_weights():
    raw_taps = [math.exp(-(offset - 4) * (offset - 4) / 4.5) for offset in range(9)]
    tap_total = sum(raw_taps)
    return [tap_value / tap_total for tap_value in raw_taps]


def lookup(indices, table):
    hits = indices[:, None] == jnp.arange(table.shape[0], dtype=jnp.int32)[None, :]
    return jnp.sum(jnp.where(hits, table[None, :], 0), axis=1)


def place(slots, values, total):
    hits = slots[None, :] == jnp.arange(total, dtype=jnp.int32)[:, None]
    return jnp.sum(jnp.where(hits, values[None, :] + 1, 0), axis=1) - 1


def same_channel(table, row_axis, column_axis):
    table = jnp.expand_dims(table, (row_axis, column_axis))
    shape = [1] * table.ndim
    shape[row_axis] = shape[column_axis] = GROUP
    return table & jnp.eye(GROUP, dtype=bool).reshape(shape)


def route_body(table_ref, cells_ref, out_ref):
    rows = cells_ref[...].reshape(-1, cells_ref.shape[-1])
    moved = jnp.dot(table_ref[...], rows, preferred_element_type=jnp.float32)
    out_ref[...] = moved.astype(out_ref.dtype).reshape(out_ref.shape)


def route(table, cells, spec, parts):
    groups = cells.shape[0] // GROUP if cells.ndim == 3 else cells.shape[1]
    rows = table.shape[0] // parts
    width = cells.shape[-1]
    return pl.pallas_call(
        route_body,
        grid=(groups,),
        in_specs=[pl.BlockSpec(table.shape, lambda g: (0, 0)), spec],
        out_specs=pl.BlockSpec((parts, 1, rows, width), lambda g: (0, g, 0, 0)),
        out_shape=jax.ShapeDtypeStruct((parts, groups, rows, width), cells.dtype),
        compiler_params=PARAMS,
    )(table, cells)


def pack(table, forward, parts):
    slots, stored = table.shape[1:]
    table = same_channel(table, 1, 3).astype(forward.dtype)
    table = table.reshape(parts * GROUP * slots, GROUP * stored)
    spec = pl.BlockSpec((GROUP,) + forward.shape[1:], lambda g: (g, 0, 0))
    return route(table, forward, spec, parts)


def row_ids(shape, slots):
    row = lax.broadcasted_iota(jnp.int32, shape, 0)
    part, inner = row // (GROUP * slots), row % (GROUP * slots)
    return part * slots + inner % slots, inner // slots


def pick_table(wanted, row_channel, per_channel):
    column = lax.broadcasted_iota(jnp.int32, row_channel.shape, 1) // per_channel
    return jnp.where(wanted & (row_channel == column), 1.0, 0.0).astype(jnp.bfloat16)


def exchange_body(src_count, vol_count, further, *refs):
    if further:
        (slots_ref, codes_ref, pool_codes_ref, notes_ref, cells_ref) = refs[:5]
        (direct_in, notes_in, rest_in) = refs[5:8]
        (direct_out, sends, receives, own, spill_out, spill_in, codes_in, rest_out) = refs[8:16]
        (pool_out, pool_in, pool_codes_in, relay_out) = refs[16:20]
        (spill_sends, spill_receives, rest_sends, rest_receives) = refs[20:]
        assert src_count == 4
    else:
        (slots_ref, notes_ref, cells_ref, direct_in, notes_in) = refs[:5]
        (direct_out, sends, receives, own) = refs[5:]
    my_src, my_vol = lax.axis_index("src"), lax.axis_index("vol")
    devices = src_count * vol_count
    me = my_src * vol_count + my_vol
    channels, stored, width = cells_ref.shape
    groups = channels // GROUP
    mesh_ids = pl.DeviceIdType.MESH

    barrier = pltpu.get_barrier_semaphore()

    def greet(step, carry):
        peer = lax.rem(me + step, devices)
        pl.semaphore_signal(
            barrier,
            inc=1,
            device_id=(peer // vol_count, lax.rem(peer, vol_count)),
            device_id_type=mesh_ids,
        )
        return carry

    lax.fori_loop(1, devices, greet, 0)

    def pack_into(out, parts, slots, row):
        shape = (parts * GROUP * slots, GROUP * stored)
        number, channel = row_ids(shape, slots)
        holders = slots_ref[row : row + 1, :]
        holders = jnp.concatenate([holders] * GROUP, axis=1)
        table = pick_table(number == holders, channel, stored)

        def pack_group(group, carry):
            cells = cells_ref[pl.ds(group * GROUP, GROUP)].reshape(GROUP * stored, width)
            moved = jnp.dot(table, cells, preferred_element_type=jnp.float32)
            out[:, group] = moved.astype(jnp.bfloat16).reshape(parts, GROUP * slots, width)
            return carry

        lax.fori_loop(0, groups, pack_group, 0)

    half = my_src // 2
    parity = lax.rem(my_src, 2)
    near = my_src + 1 - 2 * parity
    inner, outer, across = 2 - half, 3 - 3 * half, 2 - 2 * half
    is_inner = (my_src == 1) | (my_src == 2)

    def spill_copy(at, source, target, plane):
        return pltpu.make_async_remote_copy(
            src_ref=source,
            dst_ref=target,
            send_sem=spill_sends.at[at],
            recv_sem=spill_receives.at[at],
            device_id=(plane, my_vol),
            device_id_type=mesh_ids,
        )

    def near_copy():
        return spill_copy(0, spill_out.at[near], spill_in.at[my_src], near)

    def near_codes():
        return spill_copy(1, codes_ref.at[near], codes_in.at[my_src], near)

    def outer_codes(which):
        return spill_copy(2 + which, codes_ref.at[outer], codes_in.at[my_src], outer)

    def pool_copy(which):
        return spill_copy(4 + which, pool_out.at[0], pool_in.at[parity], inner)

    def pool_codes(which):
        return spill_copy(6 + which, pool_codes_ref, pool_codes_in.at[parity], inner)

    def relay_copy(which):
        return spill_copy(8 + which, relay_out.at[which], spill_in.at[across + which], near)

    def direct_copies(hop, turn):
        plane = lax.rem(my_src + hop, src_count)
        column = lax.rem(my_vol + turn, vol_count)
        peer = plane * vol_count + column
        return [
            pltpu.make_async_remote_copy(
                src_ref=source.at[peer],
                dst_ref=target.at[me],
                send_sem=sends.at[kind, hop * vol_count + turn],
                recv_sem=receives.at[kind, hop * vol_count + turn],
                device_id=(plane, column),
                device_id_type=mesh_ids,
            )
            for kind, (source, target) in enumerate(
                ((notes_ref, notes_in), (direct_out, direct_in))
            )
        ]

    def rest_copy(origin, turn):
        column = lax.rem(my_vol + turn, vol_count)
        return pltpu.make_async_remote_copy(
            src_ref=rest_out.at[origin, column],
            dst_ref=rest_in.at[origin * vol_count + my_vol],
            send_sem=rest_sends.at[origin, turn],
            recv_sem=rest_receives.at[origin, turn],
            device_id=(my_src, column),
            device_id_type=mesh_ids,
        )

    def each_turn(hop, act):
        def body(turn, carry):
            act(turn)
            return carry

        lax.fori_loop(1 if hop == 0 else 0, vol_count, body, 0)

    hops = sorted(range(src_count), key=lambda hop: (hop == 0, abs(2 * hop - src_count), hop))
    if further:
        pack_into(pool_out, 1, POOL, 2)
        pack_into(spill_out, src_count, SPILL, 1)
    pl.semaphore_wait(barrier, devices - 1)
    if further:
        pool_codes(parity).start()
        pool_copy(parity).start()
        near_codes().start()
        near_copy().start()
        outer_codes(parity).start()
    pack_into(direct_out, devices, DIRECT, 0)
    kept = [
        pltpu.make_async_copy(direct_out.at[me], direct_in.at[me], own.at[0]),
        pltpu.make_async_copy(notes_ref.at[me], notes_in.at[me], own.at[1]),
    ]

    def send_turns(first, last):
        def body(turn, carry):
            for hop in hops:
                for copy in direct_copies(hop, turn):
                    copy.start()
            return carry

        if first == 0:
            for hop in hops[:-1]:
                for copy in direct_copies(hop, 0):
                    copy.start()
        lax.fori_loop(max(first, 1), last, body, 0)

    def code_row(codes, row, slots):
        codes = codes.astype(jnp.float32)[row : row + 1, : GROUP * slots]
        return codes.astype(jnp.int32)

    def repack(code, parts, slots, held, chunk, out):
        number, channel = row_ids((parts * GROUP * slots, GROUP * held), slots)
        table = pick_table(number == code, channel, held)

        def body(group, carry):
            moved = jnp.dot(table, chunk[group], preferred_element_type=jnp.float32)
            out[:, group] = moved.astype(jnp.bfloat16).reshape(parts, GROUP * slots, width)
            return carry

        lax.fori_loop(0, groups, body, 0)

    def send_rest(origin, code, held, chunk):
        repack(code, vol_count, further, held, chunk, rest_out.at[origin])
        each_turn(0, lambda turn: rest_copy(origin, turn).start())

    if further:
        send_rest(my_src, code_row(codes_ref[my_src], 0, SPILL), SPILL, spill_out.at[my_src])
        first, second = vol_count // 2, vol_count * 3 // 4
        send_turns(0, first)
        near_codes().wait_recv()
        near_copy().wait_recv()
        send_rest(near, code_row(codes_in[near], 0, SPILL), SPILL, spill_in.at[near])

        @pl.when(is_inner)
        def _():
            for which in range(2):
                pool_codes(which).wait_recv()
                pool_copy(which).wait_recv()
                code = code_row(pool_codes_in[which], 8, POOL)
                relay = relay_out.at[pl.ds(which, 1)]
                repack(code, 1, SPILL, POOL, pool_in.at[which], relay)
                relay_copy(which).start()
            for which in range(2):
                code = code_row(pool_codes_in[which], 0, POOL)
                send_rest(across + which, code, POOL, pool_in.at[which])

        send_turns(first, second)

        @pl.when(jnp.logical_not(is_inner))
        def _():
            for which in range(2):
                origin = across + which
                outer_codes(which).wait_recv()
                relay_copy(which).wait_recv()
                send_rest(origin, code_row(codes_in[origin], 0, SPILL), SPILL, spill_in.at[origin])

        send_turns(second, vol_count)
        for origin in range(src_count):
            kept.append(
                pltpu.make_async_copy(
                    rest_out.at[origin, my_vol],
                    rest_in.at[origin * vol_count + my_vol],
                    own.at[2 + origin],
                )
            )
    else:
        send_turns(0, vol_count)
    for copy in kept:
        copy.start()
    for copy in kept:
        copy.wait()
    if further:
        pool_codes(parity).wait_send()
        pool_copy(parity).wait_send()
        near_codes().wait_send()
        near_copy().wait_send()
        outer_codes(parity).wait_send()

        @pl.when(is_inner)
        def _():
            for which in range(2):
                relay_copy(which).wait_send()

        for origin in range(src_count):
            each_turn(0, lambda turn: rest_copy(origin, turn).wait())
    for hop in hops:

        def finish(turn):
            for copy in direct_copies(hop, turn):
                copy.wait()

        each_turn(hop, finish)


def exchange(slots, codes, pool_codes, notes, cells, src_count, vol_count, further):
    channels, _, width = cells.shape
    groups = channels // GROUP
    devices = src_count * vol_count
    kind = cells.dtype
    chunk = (groups, GROUP * DIRECT, width)
    inputs = [slots] + ([codes, pool_codes] if further else []) + [notes, cells]
    outputs = [(devices,) + chunk, notes.shape] + ([(devices,) + chunk] if further else [])
    dma = pltpu.SemaphoreType.DMA
    scratch = [
        pltpu.VMEM((devices,) + chunk, kind),
        dma((2, devices)),
        dma((2, devices)),
        dma((2 + src_count,)),
    ]
    if further:
        spill = pltpu.VMEM((src_count, groups, GROUP * SPILL, width), kind)
        scratch += [spill, spill, pltpu.VMEM(codes.shape, codes.dtype)]
        scratch += [pltpu.VMEM((src_count, vol_count) + chunk, kind)]
        rows = (groups, GROUP * POOL, width)
        scratch += [pltpu.VMEM((1,) + rows, kind), pltpu.VMEM((2,) + rows, kind)]
        scratch += [pltpu.VMEM((2,) + pool_codes.shape, kind)]
        scratch += [pltpu.VMEM((2, groups, GROUP * SPILL, width), kind)]
        scratch += [dma((10,))] * 2 + [dma((src_count, vol_count))] * 2
    return pl.pallas_call(
        functools.partial(exchange_body, src_count, vol_count, further),
        in_specs=[pl.BlockSpec(memory_space=pltpu.VMEM)] * len(inputs),
        out_specs=[pl.BlockSpec(memory_space=pl.ANY)] * len(outputs),
        out_shape=[jax.ShapeDtypeStruct(shape, kind) for shape in outputs],
        scratch_shapes=scratch,
        compiler_params=pltpu.CompilerParams(
            collective_id=0, has_side_effects=True, vmem_limit_bytes=56 * 1024 * 1024
        ),
    )(*inputs)


def reduce_body(firsts, notes_ref, *refs):
    count = len(firsts)
    blocks, (adjoint_ref, out_ref, tables) = refs[:count], refs[count:]
    step = pl.program_id(0)
    local_tx, _, bricks, width = adjoint_ref.shape
    pairs = local_tx * bricks

    @pl.when(step == 0)
    def _():
        out_ref[...] = jnp.zeros_like(out_ref)
        notes = notes_ref[...].astype(jnp.float32)
        for at, first in enumerate(firsts):
            rows = notes[:, first : first + DIRECT]
            rows = jnp.concatenate([rows] * GROUP, axis=1).reshape(-1, pairs)
            rows = rows.T
            channel = lax.broadcasted_iota(jnp.int32, rows.shape, 1) // DIRECT % GROUP
            for group in range(GROUP):
                kept = jnp.where(channel == group, rows, 0.0).astype(tables.dtype)
                tables[at, group * pairs : (group + 1) * pairs] = kept

    summed = 0.0
    for at, block_ref in enumerate(blocks):
        rows = block_ref[...].reshape(-1, width)
        summed += jnp.dot(tables[at], rows, preferred_element_type=jnp.float32)
    summed = summed.reshape(GROUP, local_tx, bricks, width)
    for pair in range(GROUP // 2):
        total = 0.0
        for tx in range(local_tx):
            real = adjoint_ref[tx, 2 * pair].astype(jnp.float32)
            imag = adjoint_ref[tx, 2 * pair + 1].astype(jnp.float32)
            total += summed[2 * pair, tx] * real - summed[2 * pair + 1, tx] * imag
        vertical = lax.rem(step * (GROUP // 2) + pair, 3) == 2
        out_ref[0] += jnp.where(vertical, 0.0, total)
        out_ref[1] += jnp.where(vertical, total, 0.0)


def reduce(notes, firsts, blocks, adjoint):
    local_tx, channels, bricks, width = adjoint.shape
    sources = notes.shape[0]
    block = pl.BlockSpec((sources, 1) + blocks[0].shape[2:], lambda g: (0, g, 0, 0))
    table = (len(firsts), GROUP * local_tx * bricks, sources * GROUP * DIRECT)
    return pl.pallas_call(
        functools.partial(reduce_body, firsts),
        grid=(channels // GROUP,),
        in_specs=[pl.BlockSpec(notes.shape, lambda g: (0, 0, 0))]
        + [block] * len(blocks)
        + [pl.BlockSpec((local_tx, GROUP, bricks, width), lambda g: (0, g, 0, 0))],
        out_specs=pl.BlockSpec((2, bricks, width), lambda g: (0, 0, 0)),
        out_shape=jax.ShapeDtypeStruct((2, bricks, width), jnp.float32),
        scratch_shapes=[pltpu.VMEM(table, jnp.bfloat16)],
        compiler_params=PARAMS,
    )(notes, *blocks, adjoint)


def smooth_body(src_count, vol_count, slab_ref, out_ref, mid, low, high, done, sends, receives):
    my_src, my_vol = lax.axis_index("src"), lax.axis_index("vol")
    _, length, part_rows, columns = slab_ref.shape
    kinds, _, rows, _ = out_ref.shape
    mesh_ids = pl.DeviceIdType.MESH
    has_low, has_high = my_vol > 0, my_vol < vol_count - 1
    gather = 3

    def copies(hop, side):
        plane = lax.rem(my_src + hop, src_count)
        source, target = {
            0: (slab_ref.at[plane], mid),
            -1: (slab_ref.at[plane, pl.ds(0, HALO)], high),
            1: (slab_ref.at[plane, pl.ds(length - HALO, HALO)], low),
        }[side]
        return pltpu.make_async_remote_copy(
            src_ref=source,
            dst_ref=target.at[my_src],
            send_sem=sends.at[side + 1, hop],
            recv_sem=receives.at[side + 1, hop],
            device_id=(plane, lax.rem(my_vol + side + vol_count, vol_count)),
            device_id_type=mesh_ids,
        )

    def gather_copy(hop):
        return pltpu.make_async_remote_copy(
            src_ref=done.at[my_src],
            dst_ref=done.at[my_src],
            send_sem=sends.at[gather, hop],
            recv_sem=receives.at[gather, hop],
            device_id=(lax.rem(my_src + hop, src_count), my_vol),
            device_id_type=mesh_ids,
        )

    barrier = pltpu.get_barrier_semaphore()

    def greet(side):
        for hop in range(0 if side else 1, src_count):
            pl.semaphore_signal(
                barrier,
                inc=1,
                device_id=(lax.rem(my_src + hop, src_count), my_vol + side),
                device_id_type=mesh_ids,
            )

    greet(0)
    pl.when(has_low)(lambda: greet(-1))
    pl.when(has_high)(lambda: greet(1))
    sides = jnp.where(has_low, 1, 0) + jnp.where(has_high, 1, 0)
    pl.semaphore_wait(barrier, src_count - 1 + src_count * sides)

    def start(side):
        for hop in range(0 if side else 1, src_count):
            copies(hop, side).start()

    start(0)
    pl.when(has_low)(lambda: start(-1))
    pl.when(has_high)(lambda: start(1))
    mid[my_src] = slab_ref[my_src]

    @pl.when(jnp.logical_not(has_low))
    def _():
        low[...] = jnp.zeros_like(low)

    @pl.when(jnp.logical_not(has_high))
    def _():
        high[...] = jnp.zeros_like(high)

    weights = tap_weights()
    offset = lax.broadcasted_iota(jnp.int32, (columns, columns), 0)
    offset = offset - lax.broadcasted_iota(jnp.int32, (columns, columns), 1)
    taps = sum(
        jnp.where(offset == at - HALO, weights[at], 0.0) for at in range(2 * HALO + 1)
    )

    def arrive(side):
        for hop in range(0 if side else 1, src_count):
            copies(hop, -side).wait_recv()

    arrive(0)
    pl.when(has_low)(lambda: arrive(-1))
    pl.when(has_high)(lambda: arrive(1))
    padded = jnp.concatenate(
        [sum(part[src] for src in range(src_count)) for part in (low, mid, high)], axis=0
    )
    field = sum(weights[at] * padded[at : at + length] for at in range(2 * HALO + 1))
    field = jnp.dot(
        field.reshape(-1, columns),
        taps,
        precision=lax.Precision.HIGHEST,
        preferred_element_type=jnp.float32,
    )
    done[my_src] = field.reshape(length, part_rows, columns)
    for hop in range(1, src_count):
        gather_copy(hop).start()

    def leave(side):
        for hop in range(0 if side else 1, src_count):
            copies(hop, side).wait_send()

    leave(0)
    pl.when(has_low)(lambda: leave(-1))
    pl.when(has_high)(lambda: leave(1))
    for hop in range(1, src_count):
        gather_copy(hop).wait()
    edge = jnp.zeros((length, HALO, columns), jnp.float32)
    share = src_count // kinds
    for kind in range(kinds):
        parts = [done[kind * share + at] for at in range(share)]
        padded = jnp.concatenate([edge] + parts + [edge], axis=1)
        out_ref[kind] = sum(weights[at] * padded[:, at : at + rows] for at in range(2 * HALO + 1))


def smooth(slab, src_count, vol_count):
    length, kinds, rows, columns = slab.shape
    part = (length, kinds * rows // src_count, columns)
    slab = slab.reshape(length, src_count, part[1], columns).swapaxes(0, 1)
    whole = pltpu.VMEM((src_count,) + part, jnp.float32)
    halo = pltpu.VMEM((src_count, HALO) + part[1:], jnp.float32)
    return pl.pallas_call(
        functools.partial(smooth_body, src_count, vol_count),
        in_specs=[pl.BlockSpec(memory_space=pltpu.VMEM)],
        out_specs=pl.BlockSpec(memory_space=pltpu.VMEM),
        out_shape=jax.ShapeDtypeStruct((kinds, length, rows, columns), jnp.float32),
        scratch_shapes=[
            whole,
            halo,
            halo,
            whole,
            pltpu.SemaphoreType.DMA((4, src_count)),
            pltpu.SemaphoreType.DMA((4, src_count)),
        ],
        compiler_params=pltpu.CompilerParams(
            collective_id=1, has_side_effects=True, vmem_limit_bytes=32 * 1024 * 1024
        ),
    )(slab)


def local(forward, item_tx, item_brick, tx_place, brick_place, adjoint):
    stored = forward.shape[0]
    src_count = lax.axis_size("src")
    vol_count = lax.axis_size("vol")
    devices = src_count * vol_count
    local_tx, local_bricks = adjoint.shape[:2]
    pairs = local_tx * local_bricks
    capacity = max(2, 2 * stored // devices)
    further = DIRECT if capacity > DIRECT else 0
    ranks = DIRECT + further
    assert capacity <= 2 * DIRECT
    both = ("src", "vol")
    kind = forward.dtype

    tx_at = lookup(item_tx, tx_place)
    brick_at = lookup(item_brick, brick_place)
    plane = tx_at // local_tx
    column = brick_at // local_bricks
    owner = plane * vol_count + column
    pair = tx_at % local_tx * local_bricks + brick_at % local_bricks
    positions = jnp.arange(stored, dtype=jnp.int32)
    earlier = positions[:, None] > positions[None, :]
    rank = jnp.sum((owner[:, None] == owner[None, :]) & earlier, axis=1, dtype=jnp.int32)
    spilled = rank >= DIRECT
    before = earlier & spilled[None, :] & (plane[:, None] == plane[None, :])
    spill_rank = jnp.sum(before, axis=1, dtype=jnp.int32)
    late = spilled & (spill_rank >= SPILL)
    half = src_count // 2
    far = spilled & ~late & (plane // half != lax.axis_index("src") // half)
    pool_rank = jnp.sum(earlier & far[None, :], axis=1, dtype=jnp.int32)
    late = late | (far & (pool_rank >= POOL))
    far = far & ~late

    channel_major = forward.transpose(1, 0, 2)
    adjoint_major = adjoint.transpose(0, 2, 1, 3)

    note_rank = jnp.where(late, rank + DIRECT, rank)
    listed = place(owner * 16 + note_rank, pair, devices * 16).reshape(devices, 16)
    notes = listed[:, :, None] == jnp.arange(pairs, dtype=jnp.int32)[None, None, :]
    flag_row = jnp.arange(16, dtype=jnp.int32)[None, :, None] == 15
    notes = jnp.where(flag_row, jnp.any(late), notes).astype(kind)
    direct_slot = jnp.where(spilled, -1, owner * DIRECT + rank)
    spill_slot = jnp.where(spilled & ~late, plane * SPILL + spill_rank, -1)
    slots = jnp.zeros((8, stored), jnp.int32).at[0].set(direct_slot).at[1].set(spill_slot)
    codes = pool_codes = None
    if further:
        codes = place(spill_slot, column * further + rank - DIRECT, src_count * SPILL)
        codes = jnp.tile(codes.reshape(src_count, 1, SPILL), (1, 16, 128 // SPILL)).astype(kind)
        pool_slot = jnp.where(far, pool_rank, -1)
        slots = slots.at[2].set(pool_slot)
        is_inner = (plane == 1) | (plane == 2)
        to_rest = place(pool_slot, jnp.where(is_inner, column * further + rank - DIRECT, -1), POOL)
        to_relay = place(pool_slot, jnp.where(is_inner, -1, spill_rank), POOL)
        pool_codes = jnp.stack([to_rest, to_relay])[:, None, :]
        pool_codes = jnp.tile(pool_codes, (1, 8, 128 // POOL)).reshape(16, -1)
        pool_codes = jnp.pad(pool_codes, ((0, 0), (0, 128 - pool_codes.shape[1]))).astype(kind)
    moved = exchange(slots, codes, pool_codes, notes, channel_major, src_count, vol_count, further)
    notes = moved[1]
    firsts = (0, DIRECT) if further else (0,)
    raw = reduce(notes, firsts, [moved[0]] + list(moved[2:]), adjoint_major)

    if further:

        def late_pass():
            wanted = jnp.arange(devices * DIRECT, dtype=jnp.int32).reshape(devices, DIRECT)
            slot = jnp.where(late, owner * DIRECT + rank - DIRECT, -1)
            packed = pack(wanted[:, :, None] == slot[None, None, :], channel_major, devices)
            bricks = lax.all_to_all(packed, both, split_axis=0, concat_axis=0, tiled=True)
            return raw + reduce(notes, (2 * DIRECT,), [bricks], adjoint_major)

        raw = lax.cond(jnp.max(notes[:, 15, 0]) > 0, late_pass, lambda: raw)

    slab = raw.reshape(2, NBY, NBZ, E, E, E).transpose(3, 0, 1, 4, 2, 5)
    return smooth(slab.reshape(E, 2, NBY * E, NBZ * E), src_count, vol_count)


def solution(mesh):
    in_specs = (
        P(("src", "vol"), None, None),
        P(("src", "vol")),
        P(("src", "vol")),
        P(),
        P(),
        P("src", "vol", None, None),
    )
    out_specs = P(None, "vol", None, None)
    return jax.shard_map(local, mesh=mesh, in_specs=in_specs, out_specs=out_specs, check_vma=False)
```

```python
import functools
import math

import jax
import jax.numpy as jnp
from jax import lax
from jax.experimental import pallas as pl
from jax.experimental.pallas import tpu as pltpu
from jax.sharding import PartitionSpec as P

E = 8
NBY = 2
NBZ = 16
HALO = 4
GROUP = 4
DIRECT = 4
SPILL = 16
POOL = 20
PARAMS = pltpu.CompilerParams(vmem_limit_bytes=60 * 1024 * 1024)


def tap_weights():
    raw_taps = [math.exp(-(offset - 4) * (offset - 4) / 4.5) for offset in range(9)]
    tap_total = sum(raw_taps)
    return [tap_value / tap_total for tap_value in raw_taps]


def lookup(indices, table):
    hits = indices[:, None] == jnp.arange(table.shape[0], dtype=jnp.int32)[None, :]
    return jnp.sum(jnp.where(hits, table[None, :], 0), axis=1)


def place(slots, values, total):
    hits = slots[None, :] == jnp.arange(total, dtype=jnp.int32)[:, None]
    return jnp.sum(jnp.where(hits, values[None, :] + 1, 0), axis=1) - 1


def same_channel(table, row_axis, column_axis):
    table = jnp.expand_dims(table, (row_axis, column_axis))
    shape = [1] * table.ndim
    shape[row_axis] = shape[column_axis] = GROUP
    return table & jnp.eye(GROUP, dtype=bool).reshape(shape)


def route_body(table_ref, cells_ref, out_ref):
    rows = cells_ref[...].reshape(-1, cells_ref.shape[-1])
    moved = jnp.dot(table_ref[...], rows, preferred_element_type=jnp.float32)
    out_ref[...] = moved.astype(out_ref.dtype).reshape(out_ref.shape)


def route(table, cells, spec, parts):
    groups = cells.shape[0] // GROUP if cells.ndim == 3 else cells.shape[1]
    rows = table.shape[0] // parts
    width = cells.shape[-1]
    return pl.pallas_call(
        route_body,
        grid=(groups,),
        in_specs=[pl.BlockSpec(table.shape, lambda g: (0, 0)), spec],
        out_specs=pl.BlockSpec((parts, 1, rows, width), lambda g: (0, g, 0, 0)),
        out_shape=jax.ShapeDtypeStruct((parts, groups, rows, width), cells.dtype),
        compiler_params=PARAMS,
    )(table, cells)


def pack(table, forward, parts):
    slots, stored = table.shape[1:]
    table = same_channel(table, 1, 3).astype(forward.dtype)
    table = table.reshape(parts * GROUP * slots, GROUP * stored)
    spec = pl.BlockSpec((GROUP,) + forward.shape[1:], lambda g: (g, 0, 0))
    return route(table, forward, spec, parts)


def row_ids(shape, slots):
    row = lax.broadcasted_iota(jnp.int32, shape, 0)
    part, inner = row // (GROUP * slots), row % (GROUP * slots)
    return part * slots + inner % slots, inner // slots


def pick_table(wanted, row_channel, per_channel):
    column = lax.broadcasted_iota(jnp.int32, row_channel.shape, 1) // per_channel
    return jnp.where(wanted & (row_channel == column), 1.0, 0.0).astype(jnp.bfloat16)


def exchange_body(src_count, vol_count, further, *refs):
    if further:
        (slots_ref, codes_ref, pool_codes_ref, notes_ref, cells_ref) = refs[:5]
        (direct_in, notes_in, rest_in) = refs[5:8]
        (direct_out, sends, receives, own, spill_out, spill_in, codes_in, rest_out) = refs[8:16]
        (pool_out, pool_in, pool_codes_in, relay_out) = refs[16:20]
        (spill_sends, spill_receives, rest_sends, rest_receives) = refs[20:]
        assert src_count == 4
    else:
        (slots_ref, notes_ref, cells_ref, direct_in, notes_in) = refs[:5]
        (direct_out, sends, receives, own) = refs[5:]
    my_src, my_vol = lax.axis_index("src"), lax.axis_index("vol")
    devices = src_count * vol_count
    me = my_src * vol_count + my_vol
    channels, stored, width = cells_ref.shape
    groups = channels // GROUP
    mesh_ids = pl.DeviceIdType.MESH

    barrier = pltpu.get_barrier_semaphore()

    def greet(step, carry):
        peer = lax.rem(me + step, devices)
        pl.semaphore_signal(
            barrier,
            inc=1,
            device_id=(peer // vol_count, lax.rem(peer, vol_count)),
            device_id_type=mesh_ids,
        )
        return carry

    lax.fori_loop(1, devices, greet, 0)

    def pack_into(out, parts, slots, row):
        shape = (parts * GROUP * slots, GROUP * stored)
        number, channel = row_ids(shape, slots)
        holders = slots_ref[row : row + 1, :]
        holders = jnp.concatenate([holders] * GROUP, axis=1)
        table = pick_table(number == holders, channel, stored)

        def pack_group(group, carry):
            cells = cells_ref[pl.ds(group * GROUP, GROUP)].reshape(GROUP * stored, width)
            moved = jnp.dot(table, cells, preferred_element_type=jnp.float32)
            out[:, group] = moved.astype(jnp.bfloat16).reshape(parts, GROUP * slots, width)
            return carry

        lax.fori_loop(0, groups, pack_group, 0)

    half = my_src // 2
    parity = lax.rem(my_src, 2)
    near = my_src + 1 - 2 * parity
    inner, outer, across = 2 - half, 3 - 3 * half, 2 - 2 * half
    is_inner = (my_src == 1) | (my_src == 2)

    def spill_copy(at, source, target, plane):
        return pltpu.make_async_remote_copy(
            src_ref=source,
            dst_ref=target,
            send_sem=spill_sends.at[at],
            recv_sem=spill_receives.at[at],
            device_id=(plane, my_vol),
            device_id_type=mesh_ids,
        )

    def near_copy():
        return spill_copy(0, spill_out.at[near], spill_in.at[my_src], near)

    def near_codes():
        return spill_copy(1, codes_ref.at[near], codes_in.at[my_src], near)

    def outer_codes(which):
        return spill_copy(2 + which, codes_ref.at[outer], codes_in.at[my_src], outer)

    def pool_copy(which):
        return spill_copy(4 + which, pool_out.at[0], pool_in.at[parity], inner)

    def pool_codes(which):
        return spill_copy(6 + which, pool_codes_ref, pool_codes_in.at[parity], inner)

    def relay_copy(which):
        return spill_copy(8 + which, relay_out.at[which], spill_in.at[across + which], near)

    def direct_copies(hop, turn):
        plane = lax.rem(my_src + hop, src_count)
        column = lax.rem(my_vol + turn, vol_count)
        peer = plane * vol_count + column
        return [
            pltpu.make_async_remote_copy(
                src_ref=source.at[peer],
                dst_ref=target.at[me],
                send_sem=sends.at[kind, hop * vol_count + turn],
                recv_sem=receives.at[kind, hop * vol_count + turn],
                device_id=(plane, column),
                device_id_type=mesh_ids,
            )
            for kind, (source, target) in enumerate(
                ((notes_ref, notes_in), (direct_out, direct_in))
            )
        ]

    def rest_copy(origin, turn):
        column = lax.rem(my_vol + turn, vol_count)
        return pltpu.make_async_remote_copy(
            src_ref=rest_out.at[origin, column],
            dst_ref=rest_in.at[origin * vol_count + my_vol],
            send_sem=rest_sends.at[origin, turn],
            recv_sem=rest_receives.at[origin, turn],
            device_id=(my_src, column),
            device_id_type=mesh_ids,
        )

    def each_turn(hop, act):
        def body(turn, carry):
            act(turn)
            return carry

        lax.fori_loop(1 if hop == 0 else 0, vol_count, body, 0)

    hops = sorted(range(src_count), key=lambda hop: (hop == 0, abs(2 * hop - src_count), hop))
    if further:
        pack_into(pool_out, 1, POOL, 2)
    pl.semaphore_wait(barrier, devices - 1)
    if further:
        pool_codes(parity).start()
        pool_copy(parity).start()
        pack_into(spill_out, src_count, SPILL, 1)
        near_codes().start()
        near_copy().start()
        outer_codes(parity).start()
    pack_into(direct_out, devices, DIRECT, 0)
    kept = [
        pltpu.make_async_copy(direct_out.at[me], direct_in.at[me], own.at[0]),
        pltpu.make_async_copy(notes_ref.at[me], notes_in.at[me], own.at[1]),
    ]

    def send_turns(first, last):
        def body(turn, carry):
            for hop in hops:
                for copy in direct_copies(hop, turn):
                    copy.start()
            return carry

        if first == 0:
            for hop in hops[:-1]:
                for copy in direct_copies(hop, 0):
                    copy.start()
        lax.fori_loop(max(first, 1), last, body, 0)

    def code_row(codes, row, slots):
        codes = codes.astype(jnp.float32)[row : row + 1, : GROUP * slots]
        return codes.astype(jnp.int32)

    def repack(code, parts, slots, held, chunk, out):
        number, channel = row_ids((parts * GROUP * slots, GROUP * held), slots)
        table = pick_table(number == code, channel, held)

        def body(group, carry):
            moved = jnp.dot(table, chunk[group], preferred_element_type=jnp.float32)
            out[:, group] = moved.astype(jnp.bfloat16).reshape(parts, GROUP * slots, width)
            return carry

        lax.fori_loop(0, groups, body, 0)

    def send_rest(origin, code, held, chunk):
        repack(code, vol_count, further, held, chunk, rest_out.at[origin])
        each_turn(0, lambda turn: rest_copy(origin, turn).start())

    if further:
        send_rest(my_src, code_row(codes_ref[my_src], 0, SPILL), SPILL, spill_out.at[my_src])
        first, second = vol_count // 2, vol_count * 3 // 4
        send_turns(0, first)
        near_codes().wait_recv()
        near_copy().wait_recv()
        send_rest(near, code_row(codes_in[near], 0, SPILL), SPILL, spill_in.at[near])

        @pl.when(is_inner)
        def _():
            for which in range(2):
                pool_codes(which).wait_recv()
                pool_copy(which).wait_recv()
                code = code_row(pool_codes_in[which], 8, POOL)
                relay = relay_out.at[pl.ds(which, 1)]
                repack(code, 1, SPILL, POOL, pool_in.at[which], relay)
                relay_copy(which).start()
            for which in range(2):
                code = code_row(pool_codes_in[which], 0, POOL)
                send_rest(across + which, code, POOL, pool_in.at[which])

        send_turns(first, second)

        @pl.when(jnp.logical_not(is_inner))
        def _():
            for which in range(2):
                origin = across + which
                outer_codes(which).wait_recv()
                relay_copy(which).wait_recv()
                send_rest(origin, code_row(codes_in[origin], 0, SPILL), SPILL, spill_in.at[origin])

        send_turns(second, vol_count)
        for origin in range(src_count):
            kept.append(
                pltpu.make_async_copy(
                    rest_out.at[origin, my_vol],
                    rest_in.at[origin * vol_count + my_vol],
                    own.at[2 + origin],
                )
            )
    else:
        send_turns(0, vol_count)
    for copy in kept:
        copy.start()
    for copy in kept:
        copy.wait()
    if further:
        pool_codes(parity).wait_send()
        pool_copy(parity).wait_send()
        near_codes().wait_send()
        near_copy().wait_send()
        outer_codes(parity).wait_send()

        @pl.when(is_inner)
        def _():
            for which in range(2):
                relay_copy(which).wait_send()

        for origin in range(src_count):
            each_turn(0, lambda turn: rest_copy(origin, turn).wait())
    for hop in hops:

        def finish(turn):
            for copy in direct_copies(hop, turn):
                copy.wait()

        each_turn(hop, finish)


def exchange(slots, codes, pool_codes, notes, cells, src_count, vol_count, further):
    channels, _, width = cells.shape
    groups = channels // GROUP
    devices = src_count * vol_count
    kind = cells.dtype
    chunk = (groups, GROUP * DIRECT, width)
    inputs = [slots] + ([codes, pool_codes] if further else []) + [notes, cells]
    outputs = [(devices,) + chunk, notes.shape] + ([(devices,) + chunk] if further else [])
    dma = pltpu.SemaphoreType.DMA
    scratch = [
        pltpu.VMEM((devices,) + chunk, kind),
        dma((2, devices)),
        dma((2, devices)),
        dma((2 + src_count,)),
    ]
    if further:
        spill = pltpu.VMEM((src_count, groups, GROUP * SPILL, width), kind)
        scratch += [spill, spill, pltpu.VMEM(codes.shape, codes.dtype)]
        scratch += [pltpu.VMEM((src_count, vol_count) + chunk, kind)]
        rows = (groups, GROUP * POOL, width)
        scratch += [pltpu.VMEM((1,) + rows, kind), pltpu.VMEM((2,) + rows, kind)]
        scratch += [pltpu.VMEM((2,) + pool_codes.shape, kind)]
        scratch += [pltpu.VMEM((2, groups, GROUP * SPILL, width), kind)]
        scratch += [dma((10,))] * 2 + [dma((src_count, vol_count))] * 2
    return pl.pallas_call(
        functools.partial(exchange_body, src_count, vol_count, further),
        in_specs=[pl.BlockSpec(memory_space=pltpu.VMEM)] * len(inputs),
        out_specs=[pl.BlockSpec(memory_space=pl.ANY)] * len(outputs),
        out_shape=[jax.ShapeDtypeStruct(shape, kind) for shape in outputs],
        scratch_shapes=scratch,
        compiler_params=pltpu.CompilerParams(
            collective_id=0, has_side_effects=True, vmem_limit_bytes=56 * 1024 * 1024
        ),
    )(*inputs)


def reduce_body(firsts, notes_ref, *refs):
    count = len(firsts)
    blocks, (adjoint_ref, out_ref, tables) = refs[:count], refs[count:]
    step = pl.program_id(0)
    local_tx, _, bricks, width = adjoint_ref.shape
    pairs = local_tx * bricks

    @pl.when(step == 0)
    def _():
        out_ref[...] = jnp.zeros_like(out_ref)
        notes = notes_ref[...].astype(jnp.float32)
        for at, first in enumerate(firsts):
            rows = notes[:, first : first + DIRECT]
            rows = jnp.concatenate([rows] * GROUP, axis=1).reshape(-1, pairs)
            rows = rows.T
            channel = lax.broadcasted_iota(jnp.int32, rows.shape, 1) // DIRECT % GROUP
            for group in range(GROUP):
                kept = jnp.where(channel == group, rows, 0.0).astype(tables.dtype)
                tables[at, group * pairs : (group + 1) * pairs] = kept

    summed = 0.0
    for at, block_ref in enumerate(blocks):
        rows = block_ref[...].reshape(-1, width)
        summed += jnp.dot(tables[at], rows, preferred_element_type=jnp.float32)
    summed = summed.reshape(GROUP, local_tx, bricks, width)
    for pair in range(GROUP // 2):
        total = 0.0
        for tx in range(local_tx):
            real = adjoint_ref[tx, 2 * pair].astype(jnp.float32)
            imag = adjoint_ref[tx, 2 * pair + 1].astype(jnp.float32)
            total += summed[2 * pair, tx] * real - summed[2 * pair + 1, tx] * imag
        vertical = lax.rem(step * (GROUP // 2) + pair, 3) == 2
        out_ref[0] += jnp.where(vertical, 0.0, total)
        out_ref[1] += jnp.where(vertical, total, 0.0)


def reduce(notes, firsts, blocks, adjoint):
    local_tx, channels, bricks, width = adjoint.shape
    sources = notes.shape[0]
    block = pl.BlockSpec((sources, 1) + blocks[0].shape[2:], lambda g: (0, g, 0, 0))
    table = (len(firsts), GROUP * local_tx * bricks, sources * GROUP * DIRECT)
    return pl.pallas_call(
        functools.partial(reduce_body, firsts),
        grid=(channels // GROUP,),
        in_specs=[pl.BlockSpec(notes.shape, lambda g: (0, 0, 0))]
        + [block] * len(blocks)
        + [pl.BlockSpec((local_tx, GROUP, bricks, width), lambda g: (0, g, 0, 0))],
        out_specs=pl.BlockSpec((2, bricks, width), lambda g: (0, 0, 0)),
        out_shape=jax.ShapeDtypeStruct((2, bricks, width), jnp.float32),
        scratch_shapes=[pltpu.VMEM(table, jnp.bfloat16)],
        compiler_params=PARAMS,
    )(notes, *blocks, adjoint)


def smooth_body(src_count, vol_count, slab_ref, out_ref, mid, low, high, done, sends, receives):
    my_src, my_vol = lax.axis_index("src"), lax.axis_index("vol")
    _, length, part_rows, columns = slab_ref.shape
    kinds, _, rows, _ = out_ref.shape
    mesh_ids = pl.DeviceIdType.MESH
    has_low, has_high = my_vol > 0, my_vol < vol_count - 1
    gather = 3

    def copies(hop, side):
        plane = lax.rem(my_src + hop, src_count)
        source, target = {
            0: (slab_ref.at[plane], mid),
            -1: (slab_ref.at[plane, pl.ds(0, HALO)], high),
            1: (slab_ref.at[plane, pl.ds(length - HALO, HALO)], low),
        }[side]
        return pltpu.make_async_remote_copy(
            src_ref=source,
            dst_ref=target.at[my_src],
            send_sem=sends.at[side + 1, hop],
            recv_sem=receives.at[side + 1, hop],
            device_id=(plane, lax.rem(my_vol + side + vol_count, vol_count)),
            device_id_type=mesh_ids,
        )

    def gather_copy(hop):
        return pltpu.make_async_remote_copy(
            src_ref=done.at[my_src],
            dst_ref=done.at[my_src],
            send_sem=sends.at[gather, hop],
            recv_sem=receives.at[gather, hop],
            device_id=(lax.rem(my_src + hop, src_count), my_vol),
            device_id_type=mesh_ids,
        )

    barrier = pltpu.get_barrier_semaphore()

    def greet(side):
        for hop in range(0 if side else 1, src_count):
            pl.semaphore_signal(
                barrier,
                inc=1,
                device_id=(lax.rem(my_src + hop, src_count), my_vol + side),
                device_id_type=mesh_ids,
            )

    greet(0)
    pl.when(has_low)(lambda: greet(-1))
    pl.when(has_high)(lambda: greet(1))
    sides = jnp.where(has_low, 1, 0) + jnp.where(has_high, 1, 0)
    pl.semaphore_wait(barrier, src_count - 1 + src_count * sides)

    def start(side):
        for hop in range(0 if side else 1, src_count):
            copies(hop, side).start()

    start(0)
    pl.when(has_low)(lambda: start(-1))
    pl.when(has_high)(lambda: start(1))
    mid[my_src] = slab_ref[my_src]

    @pl.when(jnp.logical_not(has_low))
    def _():
        low[...] = jnp.zeros_like(low)

    @pl.when(jnp.logical_not(has_high))
    def _():
        high[...] = jnp.zeros_like(high)

    weights = tap_weights()
    offset = lax.broadcasted_iota(jnp.int32, (columns, columns), 0)
    offset = offset - lax.broadcasted_iota(jnp.int32, (columns, columns), 1)
    taps = sum(
        jnp.where(offset == at - HALO, weights[at], 0.0) for at in range(2 * HALO + 1)
    )

    def arrive(side):
        for hop in range(0 if side else 1, src_count):
            copies(hop, -side).wait_recv()

    arrive(0)
    pl.when(has_low)(lambda: arrive(-1))
    pl.when(has_high)(lambda: arrive(1))
    padded = jnp.concatenate(
        [sum(part[src] for src in range(src_count)) for part in (low, mid, high)], axis=0
    )
    field = sum(weights[at] * padded[at : at + length] for at in range(2 * HALO + 1))
    field = jnp.dot(
        field.reshape(-1, columns),
        taps,
        precision=lax.Precision.HIGHEST,
        preferred_element_type=jnp.float32,
    )
    done[my_src] = field.reshape(length, part_rows, columns)
    for hop in range(1, src_count):
        gather_copy(hop).start()

    def leave(side):
        for hop in range(0 if side else 1, src_count):
            copies(hop, side).wait_send()

    leave(0)
    pl.when(has_low)(lambda: leave(-1))
    pl.when(has_high)(lambda: leave(1))
    for hop in range(1, src_count):
        gather_copy(hop).wait()
    edge = jnp.zeros((length, HALO, columns), jnp.float32)
    share = src_count // kinds
    for kind in range(kinds):
        parts = [done[kind * share + at] for at in range(share)]
        padded = jnp.concatenate([edge] + parts + [edge], axis=1)
        out_ref[kind] = sum(weights[at] * padded[:, at : at + rows] for at in range(2 * HALO + 1))


def smooth(slab, src_count, vol_count):
    length, kinds, rows, columns = slab.shape
    part = (length, kinds * rows // src_count, columns)
    slab = slab.reshape(length, src_count, part[1], columns).swapaxes(0, 1)
    whole = pltpu.VMEM((src_count,) + part, jnp.float32)
    halo = pltpu.VMEM((src_count, HALO) + part[1:], jnp.float32)
    return pl.pallas_call(
        functools.partial(smooth_body, src_count, vol_count),
        in_specs=[pl.BlockSpec(memory_space=pltpu.VMEM)],
        out_specs=pl.BlockSpec(memory_space=pltpu.VMEM),
        out_shape=jax.ShapeDtypeStruct((kinds, length, rows, columns), jnp.float32),
        scratch_shapes=[
            whole,
            halo,
            halo,
            whole,
            pltpu.SemaphoreType.DMA((4, src_count)),
            pltpu.SemaphoreType.DMA((4, src_count)),
        ],
        compiler_params=pltpu.CompilerParams(
            collective_id=1, has_side_effects=True, vmem_limit_bytes=32 * 1024 * 1024
        ),
    )(slab)


def local(forward, item_tx, item_brick, tx_place, brick_place, adjoint):
    stored = forward.shape[0]
    src_count = lax.axis_size("src")
    vol_count = lax.axis_size("vol")
    devices = src_count * vol_count
    local_tx, local_bricks = adjoint.shape[:2]
    pairs = local_tx * local_bricks
    capacity = max(2, 2 * stored // devices)
    further = DIRECT if capacity > DIRECT else 0
    ranks = DIRECT + further
    assert capacity <= 2 * DIRECT
    both = ("src", "vol")
    kind = forward.dtype

    tx_at = lookup(item_tx, tx_place)
    brick_at = lookup(item_brick, brick_place)
    plane = tx_at // local_tx
    column = brick_at // local_bricks
    owner = plane * vol_count + column
    pair = tx_at % local_tx * local_bricks + brick_at % local_bricks
    positions = jnp.arange(stored, dtype=jnp.int32)
    earlier = positions[:, None] > positions[None, :]
    rank = jnp.sum((owner[:, None] == owner[None, :]) & earlier, axis=1, dtype=jnp.int32)
    spilled = rank >= DIRECT
    before = earlier & spilled[None, :] & (plane[:, None] == plane[None, :])
    spill_rank = jnp.sum(before, axis=1, dtype=jnp.int32)
    late = spilled & (spill_rank >= SPILL)
    half = src_count // 2
    far = spilled & ~late & (plane // half != lax.axis_index("src") // half)
    pool_rank = jnp.sum(earlier & far[None, :], axis=1, dtype=jnp.int32)
    late = late | (far & (pool_rank >= POOL))
    far = far & ~late

    channel_major = forward.transpose(1, 0, 2)
    adjoint_major = adjoint.transpose(0, 2, 1, 3)

    note_rank = jnp.where(late, rank + DIRECT, rank)
    listed = place(owner * 16 + note_rank, pair, devices * 16).reshape(devices, 16)
    notes = listed[:, :, None] == jnp.arange(pairs, dtype=jnp.int32)[None, None, :]
    flag_row = jnp.arange(16, dtype=jnp.int32)[None, :, None] == 15
    notes = jnp.where(flag_row, jnp.any(late), notes).astype(kind)
    direct_slot = jnp.where(spilled, -1, owner * DIRECT + rank)
    spill_slot = jnp.where(spilled & ~late, plane * SPILL + spill_rank, -1)
    slots = jnp.zeros((8, stored), jnp.int32).at[0].set(direct_slot).at[1].set(spill_slot)
    codes = pool_codes = None
    if further:
        codes = place(spill_slot, column * further + rank - DIRECT, src_count * SPILL)
        codes = jnp.tile(codes.reshape(src_count, 1, SPILL), (1, 16, 128 // SPILL)).astype(kind)
        pool_slot = jnp.where(far, pool_rank, -1)
        slots = slots.at[2].set(pool_slot)
        is_inner = (plane == 1) | (plane == 2)
        to_rest = place(pool_slot, jnp.where(is_inner, column * further + rank - DIRECT, -1), POOL)
        to_relay = place(pool_slot, jnp.where(is_inner, -1, spill_rank), POOL)
        pool_codes = jnp.stack([to_rest, to_relay])[:, None, :]
        pool_codes = jnp.tile(pool_codes, (1, 8, 128 // POOL)).reshape(16, -1)
        pool_codes = jnp.pad(pool_codes, ((0, 0), (0, 128 - pool_codes.shape[1]))).astype(kind)
    moved = exchange(slots, codes, pool_codes, notes, channel_major, src_count, vol_count, further)
    notes = moved[1]
    firsts = (0, DIRECT) if further else (0,)
    raw = reduce(notes, firsts, [moved[0]] + list(moved[2:]), adjoint_major)

    if further:

        def late_pass():
            wanted = jnp.arange(devices * DIRECT, dtype=jnp.int32).reshape(devices, DIRECT)
            slot = jnp.where(late, owner * DIRECT + rank - DIRECT, -1)
            packed = pack(wanted[:, :, None] == slot[None, None, :], channel_major, devices)
            bricks = lax.all_to_all(packed, both, split_axis=0, concat_axis=0, tiled=True)
            return raw + reduce(notes, (2 * DIRECT,), [bricks], adjoint_major)

        raw = lax.cond(jnp.max(notes[:, 15, 0]) > 0, late_pass, lambda: raw)

    slab = raw.reshape(2, NBY, NBZ, E, E, E).transpose(3, 0, 1, 4, 2, 5)
    return smooth(slab.reshape(E, 2, NBY * E, NBZ * E), src_count, vol_count)


def solution(mesh):
    in_specs = (
        P(("src", "vol"), None, None),
        P(("src", "vol")),
        P(("src", "vol")),
        P(),
        P(),
        P("src", "vol", None, None),
    )
    out_specs = P(None, "vol", None, None)
    return jax.shard_map(local, mesh=mesh, in_specs=in_specs, out_specs=out_specs, check_vma=False)
```

```python
import functools
import math

import jax
import jax.numpy as jnp
from jax import lax
from jax.experimental import pallas as pl
from jax.experimental.pallas import tpu as pltpu
from jax.sharding import PartitionSpec as P

E = 8
NBY = 2
NBZ = 16
HALO = 4
GROUP = 4
DIRECT = 4
SPILL = 16
POOL = 20
PARAMS = pltpu.CompilerParams(vmem_limit_bytes=60 * 1024 * 1024)


def tap_weights():
    raw_taps = [math.exp(-(offset - 4) * (offset - 4) / 4.5) for offset in range(9)]
    tap_total = sum(raw_taps)
    return [tap_value / tap_total for tap_value in raw_taps]


def lookup(indices, table):
    hits = indices[:, None] == jnp.arange(table.shape[0], dtype=jnp.int32)[None, :]
    return jnp.sum(jnp.where(hits, table[None, :], 0), axis=1)


def place(slots, values, total):
    hits = slots[None, :] == jnp.arange(total, dtype=jnp.int32)[:, None]
    return jnp.sum(jnp.where(hits, values[None, :] + 1, 0), axis=1) - 1


def same_channel(table, row_axis, column_axis):
    table = jnp.expand_dims(table, (row_axis, column_axis))
    shape = [1] * table.ndim
    shape[row_axis] = shape[column_axis] = GROUP
    return table & jnp.eye(GROUP, dtype=bool).reshape(shape)


def route_body(table_ref, cells_ref, out_ref):
    rows = cells_ref[...].reshape(-1, cells_ref.shape[-1])
    moved = jnp.dot(table_ref[...], rows, preferred_element_type=jnp.float32)
    out_ref[...] = moved.astype(out_ref.dtype).reshape(out_ref.shape)


def route(table, cells, spec, parts):
    groups = cells.shape[0] // GROUP if cells.ndim == 3 else cells.shape[1]
    rows = table.shape[0] // parts
    width = cells.shape[-1]
    return pl.pallas_call(
        route_body,
        grid=(groups,),
        in_specs=[pl.BlockSpec(table.shape, lambda g: (0, 0)), spec],
        out_specs=pl.BlockSpec((parts, 1, rows, width), lambda g: (0, g, 0, 0)),
        out_shape=jax.ShapeDtypeStruct((parts, groups, rows, width), cells.dtype),
        compiler_params=PARAMS,
    )(table, cells)


def pack(table, forward, parts):
    slots, stored = table.shape[1:]
    table = same_channel(table, 1, 3).astype(forward.dtype)
    table = table.reshape(parts * GROUP * slots, GROUP * stored)
    spec = pl.BlockSpec((GROUP,) + forward.shape[1:], lambda g: (g, 0, 0))
    return route(table, forward, spec, parts)


def row_ids(shape, slots):
    row = lax.broadcasted_iota(jnp.int32, shape, 0)
    part, inner = row // (GROUP * slots), row % (GROUP * slots)
    return part * slots + inner % slots, inner // slots


def pick_table(wanted, row_channel, per_channel):
    column = lax.broadcasted_iota(jnp.int32, row_channel.shape, 1) // per_channel
    return jnp.where(wanted & (row_channel == column), 1.0, 0.0).astype(jnp.bfloat16)


def exchange_body(src_count, vol_count, further, *refs):
    if further:
        (slots_ref, codes_ref, pool_codes_ref, notes_ref, cells_ref) = refs[:5]
        (direct_in, notes_in, rest_in) = refs[5:8]
        (direct_out, sends, receives, own, spill_out, spill_in, codes_in, rest_out) = refs[8:16]
        (pool_out, pool_in, pool_codes_in, relay_out) = refs[16:20]
        (spill_sends, spill_receives, rest_sends, rest_receives) = refs[20:]
        assert src_count == 4
    else:
        (slots_ref, notes_ref, cells_ref, direct_in, notes_in) = refs[:5]
        (direct_out, sends, receives, own) = refs[5:]
    my_src, my_vol = lax.axis_index("src"), lax.axis_index("vol")
    devices = src_count * vol_count
    me = my_src * vol_count + my_vol
    channels, stored, width = cells_ref.shape
    groups = channels // GROUP
    mesh_ids = pl.DeviceIdType.MESH

    barrier = pltpu.get_barrier_semaphore()

    def greet(step, carry):
        peer = lax.rem(me + step, devices)
        pl.semaphore_signal(
            barrier,
            inc=1,
            device_id=(peer // vol_count, lax.rem(peer, vol_count)),
            device_id_type=mesh_ids,
        )
        return carry

    lax.fori_loop(1, devices, greet, 0)

    def pack_into(out, parts, slots, row):
        shape = (parts * GROUP * slots, GROUP * stored)
        number, channel = row_ids(shape, slots)
        holders = slots_ref[row : row + 1, :]
        holders = jnp.concatenate([holders] * GROUP, axis=1)
        table = pick_table(number == holders, channel, stored)

        def pack_group(group, carry):
            cells = cells_ref[pl.ds(group * GROUP, GROUP)].reshape(GROUP * stored, width)
            moved = jnp.dot(table, cells, preferred_element_type=jnp.float32)
            out[:, group] = moved.astype(jnp.bfloat16).reshape(parts, GROUP * slots, width)
            return carry

        lax.fori_loop(0, groups, pack_group, 0)

    half = my_src // 2
    parity = lax.rem(my_src, 2)
    near = my_src + 1 - 2 * parity
    inner, outer, across = 2 - half, 3 - 3 * half, 2 - 2 * half
    is_inner = (my_src == 1) | (my_src == 2)

    def spill_copy(at, source, target, plane):
        return pltpu.make_async_remote_copy(
            src_ref=source,
            dst_ref=target,
            send_sem=spill_sends.at[at],
            recv_sem=spill_receives.at[at],
            device_id=(plane, my_vol),
            device_id_type=mesh_ids,
        )

    def near_copy():
        return spill_copy(0, spill_out.at[near], spill_in.at[my_src], near)

    def near_codes():
        return spill_copy(1, codes_ref.at[near], codes_in.at[my_src], near)

    def outer_codes(which):
        return spill_copy(2 + which, codes_ref.at[outer], codes_in.at[my_src], outer)

    def pool_copy(which):
        return spill_copy(4 + which, pool_out.at[0], pool_in.at[parity], inner)

    def pool_codes(which):
        return spill_copy(6 + which, pool_codes_ref, pool_codes_in.at[parity], inner)

    def relay_copy(which):
        return spill_copy(8 + which, relay_out.at[which], spill_in.at[across + which], near)

    def direct_copies(hop, turn):
        plane = lax.rem(my_src + hop, src_count)
        column = lax.rem(my_vol + turn, vol_count)
        peer = plane * vol_count + column
        return [
            pltpu.make_async_remote_copy(
                src_ref=source.at[peer],
                dst_ref=target.at[me],
                send_sem=sends.at[kind, hop * vol_count + turn],
                recv_sem=receives.at[kind, hop * vol_count + turn],
                device_id=(plane, column),
                device_id_type=mesh_ids,
            )
            for kind, (source, target) in enumerate(
                ((notes_ref, notes_in), (direct_out, direct_in))
            )
        ]

    def rest_copy(origin, turn):
        column = lax.rem(my_vol + turn, vol_count)
        return pltpu.make_async_remote_copy(
            src_ref=rest_out.at[origin, column],
            dst_ref=rest_in.at[origin * vol_count + my_vol],
            send_sem=rest_sends.at[origin, turn],
            recv_sem=rest_receives.at[origin, turn],
            device_id=(my_src, column),
            device_id_type=mesh_ids,
        )

    def each_turn(hop, act):
        def body(turn, carry):
            act(turn)
            return carry

        lax.fori_loop(1 if hop == 0 else 0, vol_count, body, 0)

    hops = sorted(range(src_count), key=lambda hop: (hop == 0, abs(2 * hop - src_count), hop))
    if further:
        pack_into(pool_out, 1, POOL, 2)
    pl.semaphore_wait(barrier, devices - 1)
    if further:
        pool_codes(parity).start()
        pool_copy(parity).start()
        pack_into(spill_out, src_count, SPILL, 1)
        near_codes().start()
        near_copy().start()
        outer_codes(parity).start()
    pack_into(direct_out, devices, DIRECT, 0)
    kept = [
        pltpu.make_async_copy(direct_out.at[me], direct_in.at[me], own.at[0]),
        pltpu.make_async_copy(notes_ref.at[me], notes_in.at[me], own.at[1]),
    ]

    def send_turns(first, last):
        def body(turn, carry):
            for hop in hops:
                for copy in direct_copies(hop, turn):
                    copy.start()
            return carry

        if first == 0:
            for hop in hops[:-1]:
                for copy in direct_copies(hop, 0):
                    copy.start()
        lax.fori_loop(max(first, 1), last, body, 0)

    def code_row(codes, row, slots):
        codes = codes.astype(jnp.float32)[row : row + 1, : GROUP * slots]
        return codes.astype(jnp.int32)

    def repack(code, parts, slots, held, chunk, out):
        number, channel = row_ids((parts * GROUP * slots, GROUP * held), slots)
        table = pick_table(number == code, channel, held)

        def body(group, carry):
            moved = jnp.dot(table, chunk[group], preferred_element_type=jnp.float32)
            out[:, group] = moved.astype(jnp.bfloat16).reshape(parts, GROUP * slots, width)
            return carry

        lax.fori_loop(0, groups, body, 0)

    def send_rest(origin, code, held, chunk):
        repack(code, vol_count, further, held, chunk, rest_out.at[origin])
        each_turn(0, lambda turn: rest_copy(origin, turn).start())

    if further:
        send_rest(my_src, code_row(codes_ref[my_src], 0, SPILL), SPILL, spill_out.at[my_src])
        first, second = vol_count * 3 // 8, vol_count * 7 // 8
        send_turns(0, first)
        near_codes().wait_recv()
        near_copy().wait_recv()
        send_rest(near, code_row(codes_in[near], 0, SPILL), SPILL, spill_in.at[near])

        @pl.when(is_inner)
        def _():
            for which in range(2):
                pool_codes(which).wait_recv()
                pool_copy(which).wait_recv()
                code = code_row(pool_codes_in[which], 8, POOL)
                relay = relay_out.at[pl.ds(which, 1)]
                repack(code, 1, SPILL, POOL, pool_in.at[which], relay)
                relay_copy(which).start()
            for which in range(2):
                code = code_row(pool_codes_in[which], 0, POOL)
                send_rest(across + which, code, POOL, pool_in.at[which])

        send_turns(first, second)

        @pl.when(jnp.logical_not(is_inner))
        def _():
            for which in range(2):
                origin = across + which
                outer_codes(which).wait_recv()
                relay_copy(which).wait_recv()
                send_rest(origin, code_row(codes_in[origin], 0, SPILL), SPILL, spill_in.at[origin])

        send_turns(second, vol_count)
        for origin in range(src_count):
            kept.append(
                pltpu.make_async_copy(
                    rest_out.at[origin, my_vol],
                    rest_in.at[origin * vol_count + my_vol],
                    own.at[2 + origin],
                )
            )
    else:
        send_turns(0, vol_count)
    for copy in kept:
        copy.start()
    for copy in kept:
        copy.wait()
    if further:
        pool_codes(parity).wait_send()
        pool_copy(parity).wait_send()
        near_codes().wait_send()
        near_copy().wait_send()
        outer_codes(parity).wait_send()

        @pl.when(is_inner)
        def _():
            for which in range(2):
                relay_copy(which).wait_send()

        for origin in range(src_count):
            each_turn(0, lambda turn: rest_copy(origin, turn).wait())
    for hop in hops:

        def finish(turn):
            for copy in direct_copies(hop, turn):
                copy.wait()

        each_turn(hop, finish)


def exchange(slots, codes, pool_codes, notes, cells, src_count, vol_count, further):
    channels, _, width = cells.shape
    groups = channels // GROUP
    devices = src_count * vol_count
    kind = cells.dtype
    chunk = (groups, GROUP * DIRECT, width)
    inputs = [slots] + ([codes, pool_codes] if further else []) + [notes, cells]
    outputs = [(devices,) + chunk, notes.shape] + ([(devices,) + chunk] if further else [])
    dma = pltpu.SemaphoreType.DMA
    scratch = [
        pltpu.VMEM((devices,) + chunk, kind),
        dma((2, devices)),
        dma((2, devices)),
        dma((2 + src_count,)),
    ]
    if further:
        spill = pltpu.VMEM((src_count, groups, GROUP * SPILL, width), kind)
        scratch += [spill, spill, pltpu.VMEM(codes.shape, codes.dtype)]
        scratch += [pltpu.VMEM((src_count, vol_count) + chunk, kind)]
        rows = (groups, GROUP * POOL, width)
        scratch += [pltpu.VMEM((1,) + rows, kind), pltpu.VMEM((2,) + rows, kind)]
        scratch += [pltpu.VMEM((2,) + pool_codes.shape, kind)]
        scratch += [pltpu.VMEM((2, groups, GROUP * SPILL, width), kind)]
        scratch += [dma((10,))] * 2 + [dma((src_count, vol_count))] * 2
    return pl.pallas_call(
        functools.partial(exchange_body, src_count, vol_count, further),
        in_specs=[pl.BlockSpec(memory_space=pltpu.VMEM)] * len(inputs),
        out_specs=[pl.BlockSpec(memory_space=pl.ANY)] * len(outputs),
        out_shape=[jax.ShapeDtypeStruct(shape, kind) for shape in outputs],
        scratch_shapes=scratch,
        compiler_params=pltpu.CompilerParams(
            collective_id=0, has_side_effects=True, vmem_limit_bytes=56 * 1024 * 1024
        ),
    )(*inputs)


def reduce_body(firsts, notes_ref, *refs):
    count = len(firsts)
    blocks, (adjoint_ref, out_ref, tables) = refs[:count], refs[count:]
    step = pl.program_id(0)
    local_tx, _, bricks, width = adjoint_ref.shape
    pairs = local_tx * bricks

    @pl.when(step == 0)
    def _():
        out_ref[...] = jnp.zeros_like(out_ref)
        notes = notes_ref[...].astype(jnp.float32)
        for at, first in enumerate(firsts):
            rows = notes[:, first : first + DIRECT]
            rows = jnp.concatenate([rows] * GROUP, axis=1).reshape(-1, pairs)
            rows = rows.T
            channel = lax.broadcasted_iota(jnp.int32, rows.shape, 1) // DIRECT % GROUP
            for group in range(GROUP):
                kept = jnp.where(channel == group, rows, 0.0).astype(tables.dtype)
                tables[at, group * pairs : (group + 1) * pairs] = kept

    summed = 0.0
    for at, block_ref in enumerate(blocks):
        rows = block_ref[...].reshape(-1, width)
        summed += jnp.dot(tables[at], rows, preferred_element_type=jnp.float32)
    summed = summed.reshape(GROUP, local_tx, bricks, width)
    for pair in range(GROUP // 2):
        total = 0.0
        for tx in range(local_tx):
            real = adjoint_ref[tx, 2 * pair].astype(jnp.float32)
            imag = adjoint_ref[tx, 2 * pair + 1].astype(jnp.float32)
            total += summed[2 * pair, tx] * real - summed[2 * pair + 1, tx] * imag
        vertical = lax.rem(step * (GROUP // 2) + pair, 3) == 2
        out_ref[0] += jnp.where(vertical, 0.0, total)
        out_ref[1] += jnp.where(vertical, total, 0.0)


def reduce(notes, firsts, blocks, adjoint):
    local_tx, channels, bricks, width = adjoint.shape
    sources = notes.shape[0]
    block = pl.BlockSpec((sources, 1) + blocks[0].shape[2:], lambda g: (0, g, 0, 0))
    table = (len(firsts), GROUP * local_tx * bricks, sources * GROUP * DIRECT)
    return pl.pallas_call(
        functools.partial(reduce_body, firsts),
        grid=(channels // GROUP,),
        in_specs=[pl.BlockSpec(notes.shape, lambda g: (0, 0, 0))]
        + [block] * len(blocks)
        + [pl.BlockSpec((local_tx, GROUP, bricks, width), lambda g: (0, g, 0, 0))],
        out_specs=pl.BlockSpec((2, bricks, width), lambda g: (0, 0, 0)),
        out_shape=jax.ShapeDtypeStruct((2, bricks, width), jnp.float32),
        scratch_shapes=[pltpu.VMEM(table, jnp.bfloat16)],
        compiler_params=PARAMS,
    )(notes, *blocks, adjoint)


def smooth_body(src_count, vol_count, slab_ref, out_ref, mid, low, high, done, sends, receives):
    my_src, my_vol = lax.axis_index("src"), lax.axis_index("vol")
    _, length, part_rows, columns = slab_ref.shape
    kinds, _, rows, _ = out_ref.shape
    mesh_ids = pl.DeviceIdType.MESH
    has_low, has_high = my_vol > 0, my_vol < vol_count - 1
    gather = 3

    def copies(hop, side):
        plane = lax.rem(my_src + hop, src_count)
        source, target = {
            0: (slab_ref.at[plane], mid),
            -1: (slab_ref.at[plane, pl.ds(0, HALO)], high),
            1: (slab_ref.at[plane, pl.ds(length - HALO, HALO)], low),
        }[side]
        return pltpu.make_async_remote_copy(
            src_ref=source,
            dst_ref=target.at[my_src],
            send_sem=sends.at[side + 1, hop],
            recv_sem=receives.at[side + 1, hop],
            device_id=(plane, lax.rem(my_vol + side + vol_count, vol_count)),
            device_id_type=mesh_ids,
        )

    def gather_copy(hop):
        return pltpu.make_async_remote_copy(
            src_ref=done.at[my_src],
            dst_ref=done.at[my_src],
            send_sem=sends.at[gather, hop],
            recv_sem=receives.at[gather, hop],
            device_id=(lax.rem(my_src + hop, src_count), my_vol),
            device_id_type=mesh_ids,
        )

    barrier = pltpu.get_barrier_semaphore()

    def greet(side):
        for hop in range(0 if side else 1, src_count):
            pl.semaphore_signal(
                barrier,
                inc=1,
                device_id=(lax.rem(my_src + hop, src_count), my_vol + side),
                device_id_type=mesh_ids,
            )

    greet(0)
    pl.when(has_low)(lambda: greet(-1))
    pl.when(has_high)(lambda: greet(1))
    sides = jnp.where(has_low, 1, 0) + jnp.where(has_high, 1, 0)
    pl.semaphore_wait(barrier, src_count - 1 + src_count * sides)

    def start(side):
        for hop in range(0 if side else 1, src_count):
            copies(hop, side).start()

    start(0)
    pl.when(has_low)(lambda: start(-1))
    pl.when(has_high)(lambda: start(1))
    mid[my_src] = slab_ref[my_src]

    @pl.when(jnp.logical_not(has_low))
    def _():
        low[...] = jnp.zeros_like(low)

    @pl.when(jnp.logical_not(has_high))
    def _():
        high[...] = jnp.zeros_like(high)

    weights = tap_weights()
    offset = lax.broadcasted_iota(jnp.int32, (columns, columns), 0)
    offset = offset - lax.broadcasted_iota(jnp.int32, (columns, columns), 1)
    taps = sum(
        jnp.where(offset == at - HALO, weights[at], 0.0) for at in range(2 * HALO + 1)
    )

    def arrive(side):
        for hop in range(0 if side else 1, src_count):
            copies(hop, -side).wait_recv()

    arrive(0)
    pl.when(has_low)(lambda: arrive(-1))
    pl.when(has_high)(lambda: arrive(1))
    padded = jnp.concatenate(
        [sum(part[src] for src in range(src_count)) for part in (low, mid, high)], axis=0
    )
    field = sum(weights[at] * padded[at : at + length] for at in range(2 * HALO + 1))
    field = jnp.dot(
        field.reshape(-1, columns),
        taps,
        precision=lax.Precision.HIGHEST,
        preferred_element_type=jnp.float32,
    )
    done[my_src] = field.reshape(length, part_rows, columns)
    for hop in range(1, src_count):
        gather_copy(hop).start()

    def leave(side):
        for hop in range(0 if side else 1, src_count):
            copies(hop, side).wait_send()

    leave(0)
    pl.when(has_low)(lambda: leave(-1))
    pl.when(has_high)(lambda: leave(1))
    for hop in range(1, src_count):
        gather_copy(hop).wait()
    edge = jnp.zeros((length, HALO, columns), jnp.float32)
    share = src_count // kinds
    for kind in range(kinds):
        parts = [done[kind * share + at] for at in range(share)]
        padded = jnp.concatenate([edge] + parts + [edge], axis=1)
        out_ref[kind] = sum(weights[at] * padded[:, at : at + rows] for at in range(2 * HALO + 1))


def smooth(slab, src_count, vol_count):
    length, kinds, rows, columns = slab.shape
    part = (length, kinds * rows // src_count, columns)
    slab = slab.reshape(length, src_count, part[1], columns).swapaxes(0, 1)
    whole = pltpu.VMEM((src_count,) + part, jnp.float32)
    halo = pltpu.VMEM((src_count, HALO) + part[1:], jnp.float32)
    return pl.pallas_call(
        functools.partial(smooth_body, src_count, vol_count),
        in_specs=[pl.BlockSpec(memory_space=pltpu.VMEM)],
        out_specs=pl.BlockSpec(memory_space=pltpu.VMEM),
        out_shape=jax.ShapeDtypeStruct((kinds, length, rows, columns), jnp.float32),
        scratch_shapes=[
            whole,
            halo,
            halo,
            whole,
            pltpu.SemaphoreType.DMA((4, src_count)),
            pltpu.SemaphoreType.DMA((4, src_count)),
        ],
        compiler_params=pltpu.CompilerParams(
            collective_id=1, has_side_effects=True, vmem_limit_bytes=32 * 1024 * 1024
        ),
    )(slab)


def local(forward, item_tx, item_brick, tx_place, brick_place, adjoint):
    stored = forward.shape[0]
    src_count = lax.axis_size("src")
    vol_count = lax.axis_size("vol")
    devices = src_count * vol_count
    local_tx, local_bricks = adjoint.shape[:2]
    pairs = local_tx * local_bricks
    capacity = max(2, 2 * stored // devices)
    further = DIRECT if capacity > DIRECT else 0
    ranks = DIRECT + further
    assert capacity <= 2 * DIRECT
    both = ("src", "vol")
    kind = forward.dtype

    tx_at = lookup(item_tx, tx_place)
    brick_at = lookup(item_brick, brick_place)
    plane = tx_at // local_tx
    column = brick_at // local_bricks
    owner = plane * vol_count + column
    pair = tx_at % local_tx * local_bricks + brick_at % local_bricks
    positions = jnp.arange(stored, dtype=jnp.int32)
    earlier = positions[:, None] > positions[None, :]
    rank = jnp.sum((owner[:, None] == owner[None, :]) & earlier, axis=1, dtype=jnp.int32)
    spilled = rank >= DIRECT
    before = earlier & spilled[None, :] & (plane[:, None] == plane[None, :])
    spill_rank = jnp.sum(before, axis=1, dtype=jnp.int32)
    late = spilled & (spill_rank >= SPILL)
    half = src_count // 2
    far = spilled & ~late & (plane // half != lax.axis_index("src") // half)
    pool_rank = jnp.sum(earlier & far[None, :], axis=1, dtype=jnp.int32)
    late = late | (far & (pool_rank >= POOL))
    far = far & ~late

    channel_major = forward.transpose(1, 0, 2)
    adjoint_major = adjoint.transpose(0, 2, 1, 3)

    note_rank = jnp.where(late, rank + DIRECT, rank)
    listed = place(owner * 16 + note_rank, pair, devices * 16).reshape(devices, 16)
    notes = listed[:, :, None] == jnp.arange(pairs, dtype=jnp.int32)[None, None, :]
    flag_row = jnp.arange(16, dtype=jnp.int32)[None, :, None] == 15
    notes = jnp.where(flag_row, jnp.any(late), notes).astype(kind)
    direct_slot = jnp.where(spilled, -1, owner * DIRECT + rank)
    spill_slot = jnp.where(spilled & ~late, plane * SPILL + spill_rank, -1)
    slots = jnp.zeros((8, stored), jnp.int32).at[0].set(direct_slot).at[1].set(spill_slot)
    codes = pool_codes = None
    if further:
        codes = place(spill_slot, column * further + rank - DIRECT, src_count * SPILL)
        codes = jnp.tile(codes.reshape(src_count, 1, SPILL), (1, 16, 128 // SPILL)).astype(kind)
        pool_slot = jnp.where(far, pool_rank, -1)
        slots = slots.at[2].set(pool_slot)
        is_inner = (plane == 1) | (plane == 2)
        to_rest = place(pool_slot, jnp.where(is_inner, column * further + rank - DIRECT, -1), POOL)
        to_relay = place(pool_slot, jnp.where(is_inner, -1, spill_rank), POOL)
        pool_codes = jnp.stack([to_rest, to_relay])[:, None, :]
        pool_codes = jnp.tile(pool_codes, (1, 8, 128 // POOL)).reshape(16, -1)
        pool_codes = jnp.pad(pool_codes, ((0, 0), (0, 128 - pool_codes.shape[1]))).astype(kind)
    moved = exchange(slots, codes, pool_codes, notes, channel_major, src_count, vol_count, further)
    notes = moved[1]
    firsts = (0, DIRECT) if further else (0,)
    raw = reduce(notes, firsts, [moved[0]] + list(moved[2:]), adjoint_major)

    if further:

        def late_pass():
            wanted = jnp.arange(devices * DIRECT, dtype=jnp.int32).reshape(devices, DIRECT)
            slot = jnp.where(late, owner * DIRECT + rank - DIRECT, -1)
            packed = pack(wanted[:, :, None] == slot[None, None, :], channel_major, devices)
            bricks = lax.all_to_all(packed, both, split_axis=0, concat_axis=0, tiled=True)
            return raw + reduce(notes, (2 * DIRECT,), [bricks], adjoint_major)

        raw = lax.cond(jnp.max(notes[:, 15, 0]) > 0, late_pass, lambda: raw)

    slab = raw.reshape(2, NBY, NBZ, E, E, E).transpose(3, 0, 1, 4, 2, 5)
    return smooth(slab.reshape(E, 2, NBY * E, NBZ * E), src_count, vol_count)


def solution(mesh):
    in_specs = (
        P(("src", "vol"), None, None),
        P(("src", "vol")),
        P(("src", "vol")),
        P(),
        P(),
        P("src", "vol", None, None),
    )
    out_specs = P(None, "vol", None, None)
    return jax.shard_map(local, mesh=mesh, in_specs=in_specs, out_specs=out_specs, check_vma=False)
```
